32 devices in a mesh: parts: 2 (over x), rows: 16 (over z, y, core).
Axes of the slice: x: 2, y: 2, z: 4, core: 2. Of those that a mesh axis runs over, the one named last changes fastest.
Arguments:
- node_features: bfloat16 [131072, 256], P(('parts', 'rows')), parts along dimension 0, may hold values from -6 to 6
- preact: bfloat16 [131072, 256], P(('parts', 'rows')), parts along dimension 0, may hold values from -6 to 6
- cotangent: bfloat16 [131072, 256], P(('parts', 'rows')), parts along dimension 0, may hold values from -6 to 6
- weight: bfloat16 [512, 256], replicated, may hold values from -0.25 to 0.25
- diag_tiles: bfloat16 [1024, 128, 128], P(('parts', 'rows')), parts along dimension 0, may hold values from 0 to 0.1796875
- edge_tiles: bfloat16 [256, 128, 128], P(('parts', 'rows')), parts along dimension 0, may hold values from 0 to 0.1796875
- entry_rows: int32 [256], P(('parts', 'rows')), parts along dimension 0, may hold values from 0 to 31
- entry_owner: int32 [256, 1], P(('parts', 'rows')), parts along dimension 0, may hold values from 0 to 15; in each aligned block of 8 rows (0 to 7, 8 to 15, ...) no two rows name the same one
- entry_cols: int32 [256], P(('parts', 'rows')), parts along dimension 0, may hold values from 0 to 31
Outputs:
- grad_nodes: bfloat16 [131072, 256], P(('parts', 'rows')), parts along dimension 0
- weight_grad: float32 [1024, 256], P('parts'), parts along dimension 0
The draws below stay inside these ranges and needn't reach their ends.
There are 2 independent parts, one for each index of `parts`. The reference program is written for one: setup_inputs(seed, part) draws one part's arguments, and reference() takes and returns one part's arrays. A program takes and returns all parts, laid end to end along the dimension named above; an argument that names none is the same for every part. Nothing has to cross between parts.
Inputs may be any that keep to these rules, and one draw needn't show every extreme that they name: `entry_owner`: among the 8 entries listed by one device no owner appears twice.
All inputs are finite; a program needn't handle non-finite values.
Results may differ from the reference program's by a relative error of at most 0.0035.
Values may be sent and summed in bfloat16 or wider, within the bound.
No kernel may reach another device: no remote copies, remote signals or barrier semaphores. Data moves between devices by JAX's collectives and lax.ppermute only.
A program may use at most 192 MiB of HBM per device.

```python
import math
import jax
import jax.numpy as jnp
import numpy as np
from jax import lax

D = 256
BS = 128
NBD = 32
REMOTE = 8
ENTRIES = 128
NB = 512
NODES = 65536
N_ROWS = 16


def touch_ends(entries, rng, low, high):
    longest = entries.shape.index(max(entries.shape))
    spots = []
    for shift in (0, 1):
        where = [jax.random.randint(jax.random.fold_in(rng, axis), (), 0, length) for axis, length in enumerate(entries.shape)]
        where[longest] = (where[longest] + shift) % entries.shape[longest]
        spots.append(tuple(where))
    return entries.at[spots[0]].set(low).at[spots[1]].set(high)


def steps_of(key, extent, shards, least, high):
    def one(axis_at, blocks):
        draws = jax.random.uniform(jax.random.fold_in(jax.random.fold_in(key, 6), axis_at), (blocks,), jnp.float32, least / len(shards), high / len(shards))
        return jnp.repeat(jnp.exp(draws), extent[axis_at] // blocks).reshape((-1,) + (1,) * (len(extent) - axis_at - 1))

    factor_of = one(*shards[0])
    for cut in shards[1:]:
        factor_of = factor_of * one(*cut)
    return factor_of


def routed_block(rng, own, number, rows, amount, top, limit, lean):
    order = jax.random.permutation(rng, amount)
    crowded, ordinary = load_shares(amount, rows * top, limit, lean, True), load_shares(amount, rows * top, limit, lean, False)
    places = jnp.arange(amount)

    def named(lengths, turn):
        used = int((lengths > 0).sum())
        fixed = max(1, used // 4)
        shifted = fixed + (places - fixed + turn * (used - fixed)) % max(1, amount - fixed)
        return jnp.zeros((amount,), jnp.int32).at[order[jnp.where(places < fixed, places, shifted)]].set(jnp.asarray(lengths, jnp.int32))

    lengths = jnp.where(number % 4 == 0, named(crowded, number // 4), named(ordinary, number - number // 4 - 1))
    mixed = jax.random.permutation(jax.random.fold_in(own, 3), amount)
    source_of, taker = mixed[0:amount // 2 * 2:2], mixed[1:amount // 2 * 2:2]
    margin = jnp.minimum(lengths[source_of] - 1, limit - lengths[taker]) // 2
    margin = jnp.where((source_of == order[0]) | (taker == order[0]) | (lengths[taker] == 0), 0, jnp.maximum(margin, 0))
    shifted = jax.random.randint(jax.random.fold_in(own, 4), (amount // 2,), 0, 1 << 20) % (margin + 1)
    lengths = lengths.at[source_of].add(-shifted).at[taker].add(shifted)
    items = jnp.searchsorted(jnp.cumsum(lengths), jnp.arange(rows * top), side="right").astype(jnp.int32)
    table = items.reshape(top, rows).T
    table = table[jax.random.permutation(jax.random.fold_in(own, 1), rows)]
    turn = jax.random.randint(jax.random.fold_in(own, 2), (rows, 1), 0, top)
    return jnp.take_along_axis(table, (jnp.arange(top)[None, :] + turn) % top, axis=1)


def load_shares(amount, total, bound, slope, full):
    weights = [(1 << 20) // math.isqrt(standing ** slope) + 1 for standing in range(1, amount + 1)]
    largest = bound if full else min(bound, max(-(-total // amount), total * weights[0] // sum(weights)))
    least = 1 if total - largest >= amount - 1 else 0
    given, rest = [largest] + [least] * (amount - 1), total - largest - least * (amount - 1)
    while rest > 0:
        free = [i for i in range(1, amount) if given[i] < largest] or [i for i in range(1, amount) if given[i] < bound]
        whole, remaining = sum([weights[i] for i in free]), rest
        for i in free:
            more = min(bound - given[i], max(1, remaining * weights[i] // whole), rest)
            given[i] = given[i] + more
            rest = rest - more
    return np.array(given)


def centred(own_key, shape, scale, bound, cuts=(), held_as=jnp.bfloat16):
    loudness = steps_of(own_key, shape, cuts, -0.22, 0.18) if cuts else 1.0
    drawn = jax.random.normal(own_key, shape, jnp.float32) * scale * loudness
    return jnp.minimum(jnp.maximum(drawn, -bound), bound).astype(held_as)


def setup_inputs(seed: int = 0, part: int = 0) -> dict:
    keys = jax.random.split(jax.random.key(seed), 10)
    own_keys = jax.random.split(jax.random.fold_in(keys[9], part), 10)
    node_features = centred(own_keys[0], (NODES, D), 1.0, 6.0, ((0, 16),))
    preact = centred(own_keys[1], (NODES, D), 1.0, 6.0, ((0, 16),))
    cotangent = centred(own_keys[2], (NODES, D), 1.0, 6.0, ((0, 16),))
    weight = centred(keys[3], (2 * D, D), (2 * D) ** -0.5, 0.25)
    diag_tiles = jnp.clip(0.1796875 * jax.random.uniform(own_keys[4], (NB, BS, BS), jnp.float32) ** steps_of(own_keys[4], (NB, BS, BS), ((0, 16),), -0.2, 0.2), 0.0, 0.1796875).astype(jnp.bfloat16)
    edge_tiles = jnp.clip(0.1796875 * jax.random.uniform(own_keys[5], (ENTRIES, BS, BS), jnp.float32) ** steps_of(own_keys[5], (ENTRIES, BS, BS), ((0, 16),), -0.2, 0.2), 0.0, 0.1796875).astype(jnp.bfloat16)
    entry_rows = touch_ends(jax.random.randint(own_keys[6], (ENTRIES,), 0, NBD), jax.random.fold_in(own_keys[6], 1), 0, NBD - 1).astype(jnp.int32)
    entry_owner_keys = jax.random.split(jax.random.fold_in(own_keys[7], 1), ENTRIES // REMOTE)
    entry_owner_turns = jax.random.permutation(jax.random.fold_in(own_keys[7], 3), ENTRIES // REMOTE)
    entry_owner = jax.vmap(lambda own, number: routed_block(jax.random.fold_in(own_keys[7], 2), own, number, REMOTE, N_ROWS, 1, 1, 2))(entry_owner_keys, entry_owner_turns).reshape((ENTRIES, 1))
    entry_cols = touch_ends(jax.random.randint(own_keys[8], (ENTRIES,), 0, NBD), jax.random.fold_in(own_keys[8], 1), 0, NBD - 1).astype(jnp.int32)
    return dict(node_features=node_features, preact=preact, cotangent=cotangent, weight=weight, diag_tiles=diag_tiles, edge_tiles=edge_tiles, entry_rows=entry_rows, entry_owner=entry_owner, entry_cols=entry_cols)


def reference(node_features, preact, cotangent, weight, diag_tiles, edge_tiles, entry_rows, entry_owner, entry_cols):
    high = lax.Precision.HIGHEST
    feat_blocks = node_features.reshape(NB, BS, D)
    grad_z = jnp.where(preact > 0, cotangent, jnp.zeros_like(cotangent))
    w_first = weight[:D]
    w_second = weight[D:]
    row_glob = jnp.arange(ENTRIES, dtype=jnp.int32) // REMOTE * NBD + entry_rows.astype(jnp.int32)
    col_glob = entry_owner[:, 0].astype(jnp.int32) * NBD + entry_cols.astype(jnp.int32)
    diag_f = diag_tiles.astype(jnp.float32)
    aggregate = jnp.einsum('bij,bjd->bid', diag_f, feat_blocks.astype(jnp.float32), precision=high)
    grad_agg = jnp.dot(grad_z, w_second.T, preferred_element_type=jnp.float32).reshape(NB, BS, D)
    backward = jnp.einsum('bji,bjd->bid', diag_f, grad_agg, precision=high)

    def advance(carry, batch):
        agg_now, back_now = carry
        tiles, rows_here, cols_here = batch
        tile_f = tiles.astype(jnp.float32)
        prods = jnp.einsum('kij,kjd->kid', tile_f, feat_blocks[cols_here].astype(jnp.float32), precision=high)
        agg_now = agg_now.at[rows_here].add(prods)
        terms = jnp.einsum('kji,kjd->kid', tile_f, grad_agg[rows_here], precision=high)
        back_now = back_now.at[cols_here].add(terms)
        return ((agg_now, back_now), None)
    batches = (edge_tiles.reshape(N_ROWS, REMOTE, BS, BS), row_glob.reshape(N_ROWS, REMOTE), col_glob.reshape(N_ROWS, REMOTE))
    (aggregate, backward), _ = lax.scan(advance, (aggregate, backward), batches)
    own_part = jnp.dot(grad_z, w_first.T, preferred_element_type=jnp.float32)
    grad_nodes = (own_part + backward.reshape(NODES, D)).astype(jnp.bfloat16)
    first = jnp.dot(node_features.T, grad_z, preferred_element_type=jnp.float32)
    second = jnp.dot(aggregate.reshape(NODES, D).T, grad_z.astype(jnp.float32), precision=high)
    factor = 1.0 / math.sqrt(NODES)
    weight_grad = jnp.concatenate([first, second], axis=0) * factor
    return (grad_nodes, weight_grad)
```

```python
import functools
import math

import jax
import jax.numpy as jnp
from jax import lax
from jax.experimental import pallas as pl
from jax.experimental.pallas import tpu as pltpu
from jax.sharding import PartitionSpec as P

F32 = jnp.float32
BF16 = jnp.bfloat16
TAG = 16
VMEM_LIMIT = 58 * 1024 * 1024

VMEM = pl.BlockSpec(memory_space=pltpu.VMEM)
SMEM = pl.BlockSpec(memory_space=pltpu.SMEM)
HBM = pl.BlockSpec(memory_space=pltpu.HBM)


def params(**more):
    return pltpu.CompilerParams(vmem_limit_bytes=VMEM_LIMIT, **more)


def loop(count, body):
    lax.fori_loop(0, count, lambda i, _: (body(i), 0)[1], 0, unroll=count <= 16)


def dot_tn(a, b):
    return lax.dot_general(a, b, (((0,), (0,)), ((), ())), preferred_element_type=F32)


def dot_nt(a, b):
    return lax.dot_general(a, b, (((1,), (1,)), ((), ())), preferred_element_type=F32)


def pack_kernel(
    rows, owner, cols, preact, cotangent, tiles, out, rows_ref, owner_ref, cols_ref, held, pre, cot, sems, late
):
    remote, size, width = pre.shape
    half = width // 2
    lists = [
        pltpu.make_async_copy(source, target, late.at[i])
        for i, (source, target) in enumerate(
            ((rows, rows_ref), (owner, owner_ref), (cols, cols_ref), (tiles, held))
        )
    ]
    for copy in lists:
        copy.start()
    lists[0].wait()

    def fetch(k):
        block = pl.ds(pl.multiple_of(rows_ref[k] * size, size), size)
        return (
            pltpu.make_async_copy(preact.at[block], pre.at[k], sems.at[0, k]),
            pltpu.make_async_copy(cotangent.at[block], cot.at[k], sems.at[1, k]),
        )

    def start(k):
        for copy in fetch(k):
            copy.start()

    loop(remote, start)
    out[...] = jnp.zeros_like(out)
    for copy in lists[1:]:
        copy.wait()

    def product(k):
        for copy in fetch(k):
            copy.wait()
        grad = jnp.where(pre[k] > 0, cot[k], jnp.zeros_like(cot[k]))
        term = dot_tn(held[k], grad).astype(BF16)
        slot = owner_ref[k]
        out[slot, 0:size, :] = term[:, :half]
        out[slot, size : 2 * size, :] = term[:, half:]
        tag = (cols_ref[k] + 1).astype(F32)
        out[slot, 2 * size :, :] = jnp.full((TAG, half), tag, F32).astype(BF16)

    loop(remote, product)


def pack(preact, cotangent, tiles, rows, owner, cols, peers):
    remote, size, _ = tiles.shape
    width = preact.shape[1]
    return pl.pallas_call(
        pack_kernel,
        out_shape=jax.ShapeDtypeStruct((peers, 2 * size + TAG, width // 2), BF16),
        in_specs=[HBM] * 6,
        out_specs=VMEM,
        scratch_shapes=[
            pltpu.SMEM((remote,), jnp.int32),
            pltpu.SMEM((remote,), jnp.int32),
            pltpu.SMEM((remote,), jnp.int32),
            pltpu.VMEM(tiles.shape, BF16),
            pltpu.VMEM((remote, size, width), BF16),
            pltpu.VMEM((remote, size, width), BF16),
            pltpu.SemaphoreType.DMA((2, remote)),
            pltpu.SemaphoreType.DMA((4,)),
        ],
        compiler_params=params(),
        name="pack",
    )(rows, owner, cols, preact, cotangent, tiles)


def local_kernel(feat, preact, cotangent, diag, weight, base, sums):
    width = feat.shape[1]
    size = diag.shape[1]
    grad = jnp.where(preact[...] > 0, cotangent[...], jnp.zeros_like(cotangent))
    parts = [dot_tn(diag[b], grad[b * size : (b + 1) * size]) for b in range(diag.shape[0])]
    adjoint = jnp.concatenate(parts, axis=0)
    high = adjoint.astype(BF16)
    low = (adjoint - high.astype(F32)).astype(BF16)
    w_first, w_second = weight[:width], weight[width:]
    base[...] = dot_nt(grad, w_first) + (dot_nt(high, w_second) + dot_nt(low, w_second))

    @pl.when(pl.program_id(0) == 0)
    def _():
        sums[...] = jnp.zeros_like(sums)

    x = feat[...]
    sums[:width] += dot_tn(x, grad)
    sums[width:] += dot_tn(x, high) + dot_tn(x, low)


def local_work(feat, preact, cotangent, diag, weight):
    nodes, width = feat.shape
    blocks, size, _ = diag.shape
    group = math.gcd(blocks, 4)
    chunk = pl.BlockSpec((group * size, width), lambda i: (i, 0))
    return pl.pallas_call(
        local_kernel,
        grid=(blocks // group,),
        out_shape=(
            jax.ShapeDtypeStruct((nodes, width), F32),
            jax.ShapeDtypeStruct((2 * width, width), F32),
        ),
        in_specs=[
            chunk,
            chunk,
            chunk,
            pl.BlockSpec((group, size, size), lambda i: (i, 0, 0)),
            pl.BlockSpec((2 * width, width), lambda i: (0, 0)),
        ],
        out_specs=(chunk, pl.BlockSpec((2 * width, width), lambda i: (0, 0))),
        compiler_params=params(dimension_semantics=("arbitrary",)),
        cost_estimate=pl.CostEstimate(
            flops=2 * nodes * width * (size + 6 * width),
            bytes_accessed=nodes * width * 10 + blocks * size * size * 2,
            transcendentals=0,
        ),
        name="local_work",
    )(feat, preact, cotangent, diag, weight)


def arrived_kernel(scale, core_ref, got, feat, sums, mine, other, ids, held, sems):
    peers, size, width = held.shape
    half = width // 2

    def fetch(p):
        block = pl.ds(pl.multiple_of(jnp.maximum(ids[p], 0) * size, size), size)
        return pltpu.make_async_copy(feat.at[block], held.at[p], sems.at[p])

    def start(p):
        tag = jnp.max(got[p, 2 * size :, :].astype(F32))
        ids[p] = tag.astype(jnp.int32) - 1
        fetch(p).start()

    loop(peers, start)
    loop(peers, lambda p: fetch(p).wait())
    group = math.gcd(peers, 16)

    def term(step, total):
        at = pl.ds(step * group, group)
        x = held[at].reshape(group * size, width)
        left = got[at, 0:size, :].reshape(group * size, half)
        right = got[at, size : 2 * size, :].reshape(group * size, half)
        return total[0] + dot_tn(x, left), total[1] + dot_tn(x, right)

    total = (sums[width:, :half], sums[width:, half:])
    total = lax.fori_loop(0, peers // group, term, total, unroll=peers == group)
    second = jnp.concatenate(total, axis=1) * scale
    first = sums[:width] * scale

    @pl.when(core_ref[0] == 0)
    def _():
        mine[...] = first
        other[...] = second

    @pl.when(core_ref[0] != 0)
    def _():
        mine[...] = second
        other[...] = first


def arrived(core, got, feat, sums, size, scale):
    peers = got.shape[0]
    width = feat.shape[1]
    return pl.pallas_call(
        functools.partial(arrived_kernel, scale),
        out_shape=(
            jax.ShapeDtypeStruct((width, width), F32),
            jax.ShapeDtypeStruct((width, width), F32),
            jax.ShapeDtypeStruct((peers,), jnp.int32),
        ),
        in_specs=[SMEM, VMEM, HBM, VMEM],
        out_specs=(VMEM, VMEM, SMEM),
        scratch_shapes=[
            pltpu.VMEM((peers, size, width), BF16),
            pltpu.SemaphoreType.DMA((peers,)),
        ],
        compiler_params=params(),
        name="arrived",
    )(core, got, feat, sums)


def finish_kernel(ids, got, base, weight, out, added):
    peers = got.shape[0]
    group, size, width = added.shape
    half = width // 2
    first = pl.program_id(0) * group
    added[...] = jnp.zeros_like(added)

    def gather(p):
        at = ids[p] - first

        @pl.when((at >= 0) & (at < group))
        def _():
            added[at, :, :half] += got[p, 0:size, :].astype(F32)
            added[at, :, half:] += got[p, size : 2 * size, :].astype(F32)

    loop(peers, gather)
    total = added[...].reshape(group * size, width).astype(BF16)
    out[...] = (base[...] + dot_nt(total, weight[width:])).astype(BF16)


def finish(ids, got, base, weight, size):
    nodes, width = base.shape
    blocks = nodes // size
    group = math.gcd(blocks, 8)
    chunk = pl.BlockSpec((group * size, width), lambda i: (i, 0))
    return pl.pallas_call(
        finish_kernel,
        grid=(blocks // group,),
        out_shape=jax.ShapeDtypeStruct((nodes, width), BF16),
        in_specs=[SMEM, VMEM, chunk, VMEM],
        out_specs=chunk,
        scratch_shapes=[pltpu.VMEM((group, size, width), F32)],
        compiler_params=params(dimension_semantics=("arbitrary",)),
        cost_estimate=pl.CostEstimate(
            flops=2 * nodes * width * width,
            bytes_accessed=nodes * width * 6,
            transcendentals=0,
        ),
        name="finish",
    )(ids, got, base, weight)


def swap(x, bit, peers):
    return lax.ppermute(x, "rows", [(i, i ^ bit) for i in range(peers)])


def sum_rows(mine, other, core, peers, grad_nodes):
    total = mine + swap(other, 1, peers)
    bit = 2
    while bit < peers:
        total = total + swap(total.astype(BF16), bit, peers).astype(F32)
        if bit == 2:
            total, grad_nodes = lax.optimization_barrier((total, grad_nodes))
        bit *= 2
    there = swap(total, 1, peers)
    first = jnp.where(core == 0, total, there)
    second = jnp.where(core == 0, there, total)
    return grad_nodes, jnp.concatenate([first, second], axis=0)


def local(
    node_features,
    preact,
    cotangent,
    weight,
    diag_tiles,
    edge_tiles,
    entry_rows,
    entry_owner,
    entry_cols,
):
    blocks, size, _ = diag_tiles.shape
    peers = lax.axis_size("rows")
    if peers & (peers - 1):
        raise ValueError("rows")
    core = lax.axis_index("rows") & 1
    scale = 1.0 / math.sqrt(peers * blocks * size)
    packed = pack(
        preact, cotangent, edge_tiles, entry_rows, entry_owner.reshape(-1), entry_cols, peers
    )
    got = lax.all_to_all(packed, "rows", split_axis=0, concat_axis=0, tiled=True)
    base, sums = local_work(node_features, preact, cotangent, diag_tiles, weight)
    mine, other, ids = arrived(
        core.reshape(1).astype(jnp.int32), got, node_features, sums, size, scale
    )
    return sum_rows(mine, other, core, peers, finish(ids, got, base, weight, size))


def solution(mesh):
    in_specs = (
        P(("parts", "rows"), None),
        P(("parts", "rows"), None),
        P(("parts", "rows"), None),
        P(),
        P(("parts", "rows"), None, None),
        P(("parts", "rows"), None, None),
        P(("parts", "rows")),
        P(("parts", "rows"), None),
        P(("parts", "rows")),
    )
    out_specs = (P(("parts", "rows"), None), P("parts", None))
    return jax.shard_map(local, mesh=mesh, in_specs=in_specs, out_specs=out_specs, check_vma=False)
```

```python
import functools
import math

import jax
import jax.numpy as jnp
from jax import lax
from jax.experimental import pallas as pl
from jax.experimental.pallas import tpu as pltpu
from jax.sharding import PartitionSpec as P

F32 = jnp.float32
BF16 = jnp.bfloat16
MIB = 1024 * 1024
TAG = 8
LOCAL_MIB = 58

VMEM = pl.BlockSpec(memory_space=pltpu.VMEM)
SMEM = pl.BlockSpec(memory_space=pltpu.SMEM)
HBM = pl.BlockSpec(memory_space=pltpu.HBM)


def params(mib):
    return pltpu.CompilerParams(vmem_limit_bytes=int(mib * MIB))


def loop(count, body):
    lax.fori_loop(0, count, lambda i, _: (body(i), 0)[1], 0, unroll=count <= 16)


def dot_tn(a, b):
    return lax.dot_general(a, b, (((0,), (0,)), ((), ())), preferred_element_type=F32)


def dot_nt(a, b):
    return lax.dot_general(a, b, (((1,), (1,)), ((), ())), preferred_element_type=F32)


def pack_kernel(
    rows, owner, cols, preact, cotangent, tiles, out,
    rows_ref, owner_ref, cols_ref, held, pre, cot, ready, blank, used, sems, late, left,
):
    remote, size, width = pre.shape
    peers = out.shape[0]
    half = width // 2
    lists = [
        pltpu.make_async_copy(source, target, late.at[i])
        for i, (source, target) in enumerate(
            ((rows, rows_ref), (owner, owner_ref), (cols, cols_ref), (tiles, held))
        )
    ]
    for copy in lists:
        copy.start()
    blank[...] = jnp.zeros_like(blank)

    def unused(p):
        used[p] = 0

    loop(peers, unused)
    lists[0].wait()

    def fetch(k):
        block = pl.ds(pl.multiple_of(rows_ref[k] * size, size), size)
        return (
            pltpu.make_async_copy(preact.at[block], pre.at[k], sems.at[0, k]),
            pltpu.make_async_copy(cotangent.at[block], cot.at[k], sems.at[1, k]),
        )

    def start(k):
        for copy in fetch(k):
            copy.start()

    loop(remote, start)
    for copy in lists[1:]:
        copy.wait()

    def mark(k):
        used[owner_ref[k]] = 1

    loop(remote, mark)

    def clear(p):
        return pltpu.make_async_copy(blank, out.at[p], left.at[p])

    def send(k):
        return pltpu.make_async_copy(ready.at[k], out.at[owner_ref[k]], left.at[peers + k])

    def start_clear(p):
        @pl.when(used[p] == 0)
        def _():
            clear(p).start()

    loop(peers, start_clear)

    def product(k):
        for copy in fetch(k):
            copy.wait()
        grad = jnp.where(pre[k] > 0, cot[k], jnp.zeros_like(cot[k]))
        term = dot_tn(held[k], grad).astype(BF16)
        ready[k, 0:size, :] = term[:, :half]
        ready[k, size : 2 * size, :] = term[:, half:]
        tag = (cols_ref[k] + 1).astype(F32)
        ready[k, 2 * size :, :] = jnp.full((TAG, half), tag, F32).astype(BF16)
        send(k).start()

    loop(remote, product)

    def end_clear(p):
        @pl.when(used[p] == 0)
        def _():
            clear(p).wait()

    loop(peers, end_clear)
    loop(remote, lambda k: send(k).wait())


def pack(preact, cotangent, tiles, rows, owner, cols, peers):
    remote, size, _ = tiles.shape
    width = preact.shape[1]
    return pl.pallas_call(
        pack_kernel,
        out_shape=jax.ShapeDtypeStruct((peers, 2 * size + TAG, width // 2), BF16),
        in_specs=[HBM] * 6,
        out_specs=HBM,
        scratch_shapes=[
            pltpu.SMEM((remote,), jnp.int32),
            pltpu.SMEM((remote,), jnp.int32),
            pltpu.SMEM((remote,), jnp.int32),
            pltpu.VMEM(tiles.shape, BF16),
            pltpu.VMEM((remote, size, width), BF16),
            pltpu.VMEM((remote, size, width), BF16),
            pltpu.VMEM((remote, 2 * size + TAG, width // 2), BF16),
            pltpu.VMEM((2 * size + TAG, width // 2), BF16),
            pltpu.SMEM((peers,), jnp.int32),
            pltpu.SemaphoreType.DMA((2, remote)),
            pltpu.SemaphoreType.DMA((4,)),
            pltpu.SemaphoreType.DMA((peers + remote,)),
        ],
        compiler_params=params(60),
        name="pack",
    )(rows, owner, cols, preact, cotangent, tiles)


def fold(x):
    half = x.shape[1] // 2
    return jnp.concatenate([x[:, :half], x[:, half:]], axis=0)


def unfold(x):
    half = x.shape[0] // 2
    return jnp.concatenate([x[:half], x[half:]], axis=1)


def two_terms(x):
    high = x.astype(BF16)
    return high, (x - high.astype(F32)).astype(BF16)


def first_kernel(group, scale, core_ref, feat, preact, cotangent, mine, other, x, pre, cot, total, came):
    width = feat.shape[1]
    span = feat.shape[0] // group

    def arrive(i):
        at = pl.ds(pl.multiple_of(i * span, span), span)
        return (
            pltpu.make_async_copy(feat.at[at], x.at[at], came.at[0, i]),
            pltpu.make_async_copy(preact.at[at], pre.at[at], came.at[1, i]),
            pltpu.make_async_copy(cotangent.at[at], cot.at[at], came.at[2, i]),
        )

    def start(i):
        for copy in arrive(i):
            copy.start()

    loop(group, start)
    total[...] = jnp.zeros_like(total)

    def step(i, _):
        at = pl.ds(pl.multiple_of(i * span, span), span)
        for copy in arrive(i):
            copy.wait()
        grad = jnp.where(pre[at] > 0, cot[at], jnp.zeros((span, width), BF16))
        total[...] += dot_tn(x[at], grad)
        return 0

    lax.fori_loop(0, group, step, 0)
    half = width // 2
    low = fold(total[:half] * scale)
    high = fold(total[half:] * scale)

    @pl.when(core_ref[0] == 0)
    def _():
        mine[...] = low
        other[...] = high

    @pl.when(core_ref[0] != 0)
    def _():
        mine[...] = high
        other[...] = low


def first_sum(scale, core, feat, preact, cotangent):
    nodes, width = feat.shape
    group = 8
    return pl.pallas_call(
        functools.partial(first_kernel, group, scale),
        out_shape=(pltpu.VMEM((width, width // 2), F32),) * 2,
        in_specs=[SMEM, HBM, HBM, HBM],
        out_specs=(VMEM, VMEM),
        scratch_shapes=[
            pltpu.VMEM((nodes, width), BF16),
            pltpu.VMEM((nodes, width), BF16),
            pltpu.VMEM((nodes, width), BF16),
            pltpu.VMEM((width, width), F32),
            pltpu.SemaphoreType.DMA((3, group)),
        ],
        compiler_params=params(60),
        cost_estimate=pl.CostEstimate(
            flops=2 * nodes * width * width,
            bytes_accessed=nodes * width * 6,
            transcendentals=0,
        ),
        name="first_sum",
    )(core, feat, preact, cotangent)


def local_kernel(group, part, scale, feat, preact, cotangent, diag, weight, *refs):
    base, nodes, turned, sums, x, pre, cot, tiles, full, rounded, total, came, left = refs[3 * part :]
    width = feat.shape[1]
    size = diag.shape[1]
    span = group * size
    steps = x.shape[0] // span
    origin = part * steps

    def here(i):
        return pl.ds(pl.multiple_of(i * span, span), span)

    def there(i):
        return here(origin + i)

    def arrive(i):
        some, same = pl.ds((origin + i) * group, group), pl.ds(i * group, group)
        return (
            pltpu.make_async_copy(preact.at[there(i)], pre.at[here(i)], came.at[0, i]),
            pltpu.make_async_copy(cotangent.at[there(i)], cot.at[here(i)], came.at[1, i]),
            pltpu.make_async_copy(diag.at[some], tiles.at[same], came.at[2, i]),
            pltpu.make_async_copy(feat.at[there(i)], x.at[here(i)], came.at[3, i]),
        )

    def leave(i):
        return (
            pltpu.make_async_copy(full.at[here(i)], base.at[there(i)], left.at[0, i]),
            pltpu.make_async_copy(rounded.at[here(i)], nodes.at[there(i)], left.at[1, i]),
        )

    def start(i):
        for copy in arrive(i):
            copy.start()

    loop(steps, start)
    total[...] = refs[0][...] if part else jnp.zeros_like(total)

    def step(i):
        at = here(i)
        for copy in arrive(i):
            copy.wait()
        grad = jnp.where(pre[at] > 0, cot[at], jnp.zeros((span, width), BF16))
        parts = [
            dot_tn(tiles[i * group + b], grad[b * size : (b + 1) * size]) for b in range(group)
        ]
        high, low = two_terms(jnp.concatenate(parts, axis=0))
        w_first, w_second = weight[:width], weight[width:]
        own = dot_nt(grad, w_first) + (dot_nt(high, w_second) + dot_nt(low, w_second))
        full[at] = own
        rounded[at] = own.astype(BF16)
        columns = x[at].T
        for b in range(group):
            turned[i * group + b] = columns[:, b * size : (b + 1) * size]
        for copy in leave(i):
            copy.start()
        total[...] += jnp.dot(columns, high, preferred_element_type=F32) + jnp.dot(
            columns, low, preferred_element_type=F32
        )

    lax.fori_loop(0, steps, lambda i, _: (step(i), 0)[1], 0)
    sums[...] = total[...] * scale if part else total[...]

    def drain(i):
        for copy in leave(i):
            copy.wait()

    loop(steps, drain)


def local_work(scale, feat, preact, cotangent, diag, weight, *state):
    part = 1 if state else 0
    rows, width = feat.shape
    blocks, size, _ = diag.shape
    group = math.gcd(blocks // 2, 4)
    steps = blocks // 2 // group
    return pl.pallas_call(
        functools.partial(local_kernel, group, part, scale),
        out_shape=(
            jax.ShapeDtypeStruct((rows, width), F32),
            jax.ShapeDtypeStruct((rows, width), BF16),
            pltpu.VMEM((blocks // 2, width, size), BF16),
            pltpu.VMEM((width, width), F32),
        ),
        in_specs=[HBM, HBM, HBM, HBM, VMEM] + [VMEM, HBM, HBM][: len(state)],
        out_specs=(HBM, HBM, VMEM, VMEM),
        scratch_shapes=[
            pltpu.VMEM((rows // 2, width), BF16),
            pltpu.VMEM((rows // 2, width), BF16),
            pltpu.VMEM((rows // 2, width), BF16),
            pltpu.VMEM((blocks // 2, size, size), BF16),
            pltpu.VMEM((rows // 2, width), F32),
            pltpu.VMEM((rows // 2, width), BF16),
            pltpu.VMEM((width, width), F32),
            pltpu.SemaphoreType.DMA((4, steps)),
            pltpu.SemaphoreType.DMA((2, steps)),
        ],
        input_output_aliases={6: 0, 7: 1} if part else {},
        compiler_params=params(LOCAL_MIB),
        cost_estimate=pl.CostEstimate(
            flops=rows * width * (size + 5 * width),
            bytes_accessed=rows * width * 7 + blocks * size * size,
            transcendentals=0,
        ),
        name="local_work",
    )(feat, preact, cotangent, diag, weight, *state)


def arrived_kernel(scale, core_ref, got, low_blocks, high_blocks, sums, mine, other, ids):
    peers = got.shape[0]
    half, width, size = low_blocks.shape
    group = math.gcd(peers, 16)

    def mark(p):
        ids[p] = jnp.max(got[p, 2 * size :, :].astype(F32)).astype(jnp.int32) - 1

    loop(peers, mark)

    def block(p):
        at = ids[p]
        low = low_blocks[jnp.clip(at, 0, half - 1)]
        high = high_blocks[jnp.maximum(at - half, 0)]
        return jnp.where(at < half, low, high)

    def term(step, total):
        for q in range(0, group, 2):
            pair = (step * group + q, step * group + q + 1)
            left = jnp.concatenate([block(p) for p in pair], axis=1)
            right = jnp.concatenate([unfold(got[p, : 2 * size, :]) for p in pair], axis=0)
            total = total + jnp.dot(left, right, preferred_element_type=F32)
        return total

    total = jnp.zeros((width, width), F32)
    total = lax.fori_loop(0, peers // group, term, total, unroll=peers == group)
    total = total * scale + sums[...]
    low, high = fold(total[: width // 2]), fold(total[width // 2 :])

    @pl.when(core_ref[0] == 0)
    def _():
        mine[...] = low
        other[...] = high

    @pl.when(core_ref[0] != 0)
    def _():
        mine[...] = high
        other[...] = low


def arrived(core, got, low_blocks, high_blocks, sums, scale):
    peers = got.shape[0]
    _, width, size = low_blocks.shape
    return pl.pallas_call(
        functools.partial(arrived_kernel, scale),
        out_shape=(pltpu.VMEM((width, width // 2), F32),) * 2
        + (jax.ShapeDtypeStruct((peers,), jnp.int32),),
        in_specs=[SMEM, VMEM, VMEM, VMEM, VMEM],
        out_specs=(VMEM, VMEM, SMEM),
        compiler_params=params(8 + peers * size * width * 5 / MIB),
        name="arrived",
    )(core, got, low_blocks, high_blocks, sums)


def finish_kernel(ids, got, weight, base, nodes, out, near, ready, terms, last, count, came, left):
    peers, size, width = near.shape
    half = width // 2

    def block(p):
        return pl.ds(pl.multiple_of(ids[p] * size, size), size)

    def read(p):
        return pltpu.make_async_copy(base.at[block(p)], near.at[p], came.at[p])

    def write(p):
        return pltpu.make_async_copy(ready.at[p], out.at[block(p)], left.at[p])

    def writes(p):
        return (ids[p] >= 0) & (last[jnp.maximum(ids[p], 0)] == p)

    def clear(b):
        count[b] = 0

    loop(last.shape[0], clear)

    def tally(p):
        @pl.when(ids[p] >= 0)
        def _():
            last[ids[p]] = p
            count[ids[p]] += 1

    loop(peers, tally)

    def start(p):
        @pl.when(writes(p))
        def _():
            read(p).start()

    loop(peers, start)
    group = math.gcd(peers, 16)

    def product(step):
        at = pl.ds(step * group, group)
        tile = jnp.concatenate([got[at, :size, :], got[at, size : 2 * size, :]], axis=2)
        tile = tile.reshape(group * size, width)
        terms[at] = dot_nt(tile, weight[width:]).reshape(group, size, width)

    loop(peers // group, product)

    def one(p):
        @pl.when(writes(p))
        def _():
            read(p).wait()

            @pl.when(count[ids[p]] > 1)
            def _():
                def add(q, _):
                    @pl.when(ids[q] == ids[p])
                    def _():
                        near[p] += terms[q]

                    return 0

                lax.fori_loop(0, p, add, 0)

            ready[p] = (near[p] + terms[p]).astype(BF16)
            write(p).start()

    def drain(p):
        @pl.when(writes(p))
        def _():
            write(p).wait()

    loop(peers, one)
    loop(peers, drain)


def finish(ids, got, weight, base, nodes, size):
    peers = got.shape[0]
    width = base.shape[1]
    return pl.pallas_call(
        finish_kernel,
        out_shape=jax.ShapeDtypeStruct(nodes.shape, BF16),
        in_specs=[SMEM, VMEM, VMEM, HBM, HBM],
        out_specs=HBM,
        scratch_shapes=[
            pltpu.VMEM((peers, size, width), F32),
            pltpu.VMEM((peers, size, width), BF16),
            pltpu.VMEM((peers, size, width), F32),
            pltpu.SMEM((nodes.shape[0] // size,), jnp.int32),
            pltpu.SMEM((nodes.shape[0] // size,), jnp.int32),
            pltpu.SemaphoreType.DMA((peers,)),
            pltpu.SemaphoreType.DMA((peers,)),
        ],
        input_output_aliases={4: 0},
        compiler_params=params(60),
        cost_estimate=pl.CostEstimate(
            flops=2 * peers * size * width * width,
            bytes_accessed=peers * size * width * 8,
            transcendentals=0,
        ),
        name="finish",
    )(ids, got, weight, base, nodes)


def swap(x, bit, peers):
    return lax.ppermute(x, "rows", [(i, i ^ bit) for i in range(peers)])


def widen(total, core, peers):
    there = swap(total, 1, peers)
    low, high = jnp.where(core == 0, total, there), jnp.where(core == 0, there, total)
    half = total.shape[0] // 2
    return [jnp.concatenate([x[:half], x[half:]], axis=1) for x in (low, high)]


def exchange(total, bit, peers):
    return total + swap(total.astype(BF16), bit, peers).astype(F32)


def local(
    node_features,
    preact,
    cotangent,
    weight,
    diag_tiles,
    edge_tiles,
    entry_rows,
    entry_owner,
    entry_cols,
):
    blocks, size, _ = diag_tiles.shape
    peers = lax.axis_size("rows")
    if peers & (peers - 1):
        raise ValueError("rows")
    core = lax.axis_index("rows") & 1
    which = core.reshape(1).astype(jnp.int32)
    scale = 1.0 / math.sqrt(peers * blocks * size)
    bits = [1 << i for i in range(1, peers.bit_length() - 1)]
    packed = pack(
        preact, cotangent, edge_tiles, entry_rows, entry_owner.reshape(-1), entry_cols, peers
    )
    got = lax.all_to_all(packed, "rows", split_axis=0, concat_axis=0, tiled=True)

    mine, other = first_sum(scale, which, node_features, preact, cotangent)
    first = mine + swap(other, 1, peers)
    arrays = (node_features, preact, cotangent, diag_tiles, weight)
    base, nodes, low_blocks, sums = local_work(scale, *arrays)
    for bit in bits[:-1]:
        first = exchange(first, bit, peers)
        if bit == 2:
            first, sums = lax.optimization_barrier((first, sums))
    base, nodes, high_blocks, sums = local_work(scale, *arrays, sums, base, nodes)
    first, sums = lax.optimization_barrier((first, sums))

    first, got = lax.optimization_barrier((first, got))
    mine, other, ids = arrived(which, got, low_blocks, high_blocks, sums, scale)
    second = mine + swap(other, 1, peers)
    for bit in bits[-1:]:
        first = exchange(first, bit, peers)
    for bit in bits[:-1]:
        second = exchange(second, bit, peers)
    tied, second = lax.optimization_barrier((ids, second))
    nodes = finish(tied, got, weight, base, nodes, size)
    for bit in bits[-1:]:
        second = exchange(second, bit, peers)
    second, nodes = lax.optimization_barrier((second, nodes))
    rows = widen(first, core, peers) + widen(second, core, peers)
    return nodes, jnp.concatenate(rows, axis=0)


def solution(mesh):
    in_specs = (
        P(("parts", "rows"), None),
        P(("parts", "rows"), None),
        P(("parts", "rows"), None),
        P(),
        P(("parts", "rows"), None, None),
        P(("parts", "rows"), None, None),
        P(("parts", "rows")),
        P(("parts", "rows"), None),
        P(("parts", "rows")),
    )
    out_specs = (P(("parts", "rows"), None), P("parts", None))
    return jax.shard_map(local, mesh=mesh, in_specs=in_specs, out_specs=out_specs, check_vma=False)
```

```python
import functools
import math

import jax
import jax.numpy as jnp
from jax import lax
from jax.experimental import pallas as pl
from jax.experimental.pallas import tpu as pltpu
from jax.sharding import PartitionSpec as P

F32 = jnp.float32
BF16 = jnp.bfloat16
MIB = 1024 * 1024
TAG = 8
PACK_GROUP = 4
LOCAL_MIB = 58

VMEM = pl.BlockSpec(memory_space=pltpu.VMEM)
SMEM = pl.BlockSpec(memory_space=pltpu.SMEM)
HBM = pl.BlockSpec(memory_space=pltpu.HBM)


def in_hbm(*arrays):
    return [pltpu.with_memory_space_constraint(x, pltpu.HBM) for x in arrays]


def params(mib):
    return pltpu.CompilerParams(vmem_limit_bytes=int(mib * MIB))


def loop(count, body):
    lax.fori_loop(0, count, lambda i, _: (body(i), 0)[1], 0, unroll=count <= 16)


def dot_tn(a, b):
    return lax.dot_general(a, b, (((0,), (0,)), ((), ())), preferred_element_type=F32)


def dot_nt(a, b):
    return lax.dot_general(a, b, (((1,), (1,)), ((), ())), preferred_element_type=F32)


def pack_kernel(
    rows, owner, cols, preact, cotangent, tiles, out,
    rows_ref, owner_ref, cols_ref, held, pre, cot, ready, blank, used, sems, late, left,
):
    remote, size, width = pre.shape
    peers = out.shape[0]
    half = width // 2
    lists = [
        pltpu.make_async_copy(source, target, late.at[i])
        for i, (source, target) in enumerate(
            ((rows, rows_ref), (owner, owner_ref), (cols, cols_ref), (tiles, held))
        )
    ]
    for copy in lists:
        copy.start()
    blank[...] = jnp.zeros_like(blank)

    def unused(p):
        used[p] = 0

    loop(peers, unused)
    lists[0].wait()

    def fetch(k):
        block = pl.ds(pl.multiple_of(rows_ref[k] * size, size), size)
        return (
            pltpu.make_async_copy(preact.at[block], pre.at[k], sems.at[0, k]),
            pltpu.make_async_copy(cotangent.at[block], cot.at[k], sems.at[1, k]),
        )

    def start(k):
        for copy in fetch(k):
            copy.start()

    loop(remote, start)
    for copy in lists[1:]:
        copy.wait()

    def turn(k):
        held[k] = held[k].T

    loop(remote, turn)

    def mark(k):
        used[owner_ref[k]] = 1

    loop(remote, mark)

    def clear(p):
        return pltpu.make_async_copy(blank, out.at[p], left.at[p])

    def send(k):
        return pltpu.make_async_copy(ready.at[k], out.at[owner_ref[k]], left.at[peers + k])

    def start_clear(p):
        @pl.when(used[p] == 0)
        def _():
            clear(p).start()

    loop(peers, start_clear)

    def product(k):
        grad = jnp.where(pre[k] > 0, cot[k], jnp.zeros_like(cot[k]))
        term = jnp.dot(held[k], grad, preferred_element_type=F32).astype(BF16)
        ready[k, 0:size, :] = term[:, :half]
        ready[k, size : 2 * size, :] = term[:, half:]
        tag = (cols_ref[k] + 1).astype(F32)
        ready[k, 2 * size :, :] = jnp.full((TAG, half), tag, F32).astype(BF16)

    group = math.gcd(remote, PACK_GROUP)

    def batch(step):
        for k in range(group):
            for copy in fetch(step * group + k):
                copy.wait()
        for k in range(group):
            product(step * group + k)
        for k in range(group):
            send(step * group + k).start()

    loop(remote // group, batch)

    def end_clear(p):
        @pl.when(used[p] == 0)
        def _():
            clear(p).wait()

    loop(peers, end_clear)
    loop(remote, lambda k: send(k).wait())


def pack(preact, cotangent, tiles, rows, owner, cols, peers):
    remote, size, _ = tiles.shape
    width = preact.shape[1]
    return pl.pallas_call(
        pack_kernel,
        out_shape=jax.ShapeDtypeStruct((peers, 2 * size + TAG, width // 2), BF16),
        in_specs=[HBM] * 6,
        out_specs=HBM,
        scratch_shapes=[
            pltpu.SMEM((remote,), jnp.int32),
            pltpu.SMEM((remote,), jnp.int32),
            pltpu.SMEM((remote,), jnp.int32),
            pltpu.VMEM(tiles.shape, BF16),
            pltpu.VMEM((remote, size, width), BF16),
            pltpu.VMEM((remote, size, width), BF16),
            pltpu.VMEM((remote, 2 * size + TAG, width // 2), BF16),
            pltpu.VMEM((2 * size + TAG, width // 2), BF16),
            pltpu.SMEM((peers,), jnp.int32),
            pltpu.SemaphoreType.DMA((2, remote)),
            pltpu.SemaphoreType.DMA((4,)),
            pltpu.SemaphoreType.DMA((peers + remote,)),
        ],
        compiler_params=params(60),
        name="pack",
    )(*in_hbm(rows, owner, cols, preact, cotangent, tiles))


def fold(x):
    half = x.shape[1] // 2
    return jnp.concatenate([x[:, :half], x[:, half:]], axis=0)


def unfold(x):
    half = x.shape[0] // 2
    return jnp.concatenate([x[:half], x[half:]], axis=1)


def two_terms(x):
    high = x.astype(BF16)
    return high, (x - high.astype(F32)).astype(BF16)


def first_kernel(group, scale, core_ref, feat, preact, cotangent, mine, other, x, pre, cot, total, came):
    width = feat.shape[1]
    span = feat.shape[0] // group

    def arrive(i):
        at = pl.ds(pl.multiple_of(i * span, span), span)
        return (
            pltpu.make_async_copy(feat.at[at], x.at[at], came.at[0, i]),
            pltpu.make_async_copy(preact.at[at], pre.at[at], came.at[1, i]),
            pltpu.make_async_copy(cotangent.at[at], cot.at[at], came.at[2, i]),
        )

    def start(i):
        for copy in arrive(i):
            copy.start()

    loop(group, start)
    total[...] = jnp.zeros_like(total)

    def step(i, _):
        at = pl.ds(pl.multiple_of(i * span, span), span)
        for copy in arrive(i):
            copy.wait()
        grad = jnp.where(pre[at] > 0, cot[at], jnp.zeros((span, width), BF16))
        total[...] += dot_tn(x[at], grad)
        return 0

    lax.fori_loop(0, group, step, 0)
    half = width // 2
    low = fold(total[:half] * scale)
    high = fold(total[half:] * scale)

    @pl.when(core_ref[0] == 0)
    def _():
        mine[...] = low
        other[...] = high

    @pl.when(core_ref[0] != 0)
    def _():
        mine[...] = high
        other[...] = low


def first_sum(scale, core, feat, preact, cotangent):
    nodes, width = feat.shape
    group = 8
    return pl.pallas_call(
        functools.partial(first_kernel, group, scale),
        out_shape=(pltpu.VMEM((width, width // 2), F32),) * 2,
        in_specs=[SMEM, HBM, HBM, HBM],
        out_specs=(VMEM, VMEM),
        scratch_shapes=[
            pltpu.VMEM((nodes, width), BF16),
            pltpu.VMEM((nodes, width), BF16),
            pltpu.VMEM((nodes, width), BF16),
            pltpu.VMEM((width, width), F32),
            pltpu.SemaphoreType.DMA((3, group)),
        ],
        compiler_params=params(60),
        cost_estimate=pl.CostEstimate(
            flops=2 * nodes * width * width,
            bytes_accessed=nodes * width * 6,
            transcendentals=0,
        ),
        name="first_sum",
    )(core, *in_hbm(feat, preact, cotangent))


def local_kernel(group, part, scale, feat, preact, cotangent, diag, weight, *refs):
    base, nodes, turned, sums, x, pre, cot, tiles, full, rounded, total, came, left = refs[3 * part :]
    width = feat.shape[1]
    size = diag.shape[1]
    span = group * size
    steps = x.shape[0] // span
    origin = part * steps

    def here(i):
        return pl.ds(pl.multiple_of(i * span, span), span)

    def there(i):
        return here(origin + i)

    def arrive(i):
        some, same = pl.ds((origin + i) * group, group), pl.ds(i * group, group)
        return (
            pltpu.make_async_copy(preact.at[there(i)], pre.at[here(i)], came.at[0, i]),
            pltpu.make_async_copy(cotangent.at[there(i)], cot.at[here(i)], came.at[1, i]),
            pltpu.make_async_copy(diag.at[some], tiles.at[same], came.at[2, i]),
            pltpu.make_async_copy(feat.at[there(i)], x.at[here(i)], came.at[3, i]),
        )

    def leave(i):
        return (
            pltpu.make_async_copy(full.at[here(i)], base.at[there(i)], left.at[0, i]),
            pltpu.make_async_copy(rounded.at[here(i)], nodes.at[there(i)], left.at[1, i]),
        )

    def start(i):
        for copy in arrive(i):
            copy.start()

    loop(steps, start)
    total[...] = refs[0][...] if part else jnp.zeros_like(total)

    def step(i):
        at = here(i)
        for copy in arrive(i):
            copy.wait()
        grad = jnp.where(pre[at] > 0, cot[at], jnp.zeros((span, width), BF16))
        parts = [
            dot_tn(tiles[i * group + b], grad[b * size : (b + 1) * size]) for b in range(group)
        ]
        high, low = two_terms(jnp.concatenate(parts, axis=0))
        w_first, w_second = weight[:width], weight[width:]
        own = dot_nt(grad, w_first) + (dot_nt(high, w_second) + dot_nt(low, w_second))
        full[at] = own
        rounded[at] = own.astype(BF16)
        columns = x[at].T
        for b in range(group):
            turned[i * group + b] = columns[:, b * size : (b + 1) * size]
        for copy in leave(i):
            copy.start()
        total[...] += jnp.dot(columns, high, preferred_element_type=F32) + jnp.dot(
            columns, low, preferred_element_type=F32
        )

    lax.fori_loop(0, steps, lambda i, _: (step(i), 0)[1], 0)
    sums[...] = total[...] * scale if part else total[...]

    def drain(i):
        for copy in leave(i):
            copy.wait()

    loop(steps, drain)


def local_work(scale, feat, preact, cotangent, diag, weight, *state):
    part = 1 if state else 0
    rows, width = feat.shape
    blocks, size, _ = diag.shape
    group = math.gcd(blocks // 2, 4)
    steps = blocks // 2 // group
    return pl.pallas_call(
        functools.partial(local_kernel, group, part, scale),
        out_shape=(
            pltpu.HBM((rows, width), F32),
            pltpu.HBM((rows, width), BF16),
            pltpu.VMEM((blocks // 2, width, size), BF16),
            pltpu.VMEM((width, width), F32),
        ),
        in_specs=[HBM, HBM, HBM, HBM, VMEM] + [VMEM, HBM, HBM][: len(state)],
        out_specs=(HBM, HBM, VMEM, VMEM),
        scratch_shapes=[
            pltpu.VMEM((rows // 2, width), BF16),
            pltpu.VMEM((rows // 2, width), BF16),
            pltpu.VMEM((rows // 2, width), BF16),
            pltpu.VMEM((blocks // 2, size, size), BF16),
            pltpu.VMEM((rows // 2, width), F32),
            pltpu.VMEM((rows // 2, width), BF16),
            pltpu.VMEM((width, width), F32),
            pltpu.SemaphoreType.DMA((4, steps)),
            pltpu.SemaphoreType.DMA((2, steps)),
        ],
        input_output_aliases={6: 0, 7: 1} if part else {},
        compiler_params=params(LOCAL_MIB),
        cost_estimate=pl.CostEstimate(
            flops=rows * width * (size + 5 * width),
            bytes_accessed=rows * width * 7 + blocks * size * size,
            transcendentals=0,
        ),
        name="local_work",
    )(*in_hbm(feat, preact, cotangent, diag), weight, *state[:1], *in_hbm(*state[1:]))


def arrived_kernel(scale, core_ref, got, low_blocks, high_blocks, sums, mine, other, ids):
    peers = got.shape[0]
    half, width, size = low_blocks.shape
    group = math.gcd(peers, 16)

    def mark(p):
        ids[p] = jnp.max(got[p, 2 * size :, :].astype(F32)).astype(jnp.int32) - 1

    loop(peers, mark)

    def block(p):
        at = ids[p]
        low = low_blocks[jnp.clip(at, 0, half - 1)]
        high = high_blocks[jnp.maximum(at - half, 0)]
        return jnp.where(at < half, low, high)

    def term(step, total):
        for q in range(0, group, 2):
            pair = (step * group + q, step * group + q + 1)
            left = jnp.concatenate([block(p) for p in pair], axis=1)
            right = jnp.concatenate([unfold(got[p, : 2 * size, :]) for p in pair], axis=0)
            total = total + jnp.dot(left, right, preferred_element_type=F32)
        return total

    total = jnp.zeros((width, width), F32)
    total = lax.fori_loop(0, peers // group, term, total, unroll=peers == group)
    total = total * scale + sums[...]
    low, high = fold(total[: width // 2]), fold(total[width // 2 :])

    @pl.when(core_ref[0] == 0)
    def _():
        mine[...] = low
        other[...] = high

    @pl.when(core_ref[0] != 0)
    def _():
        mine[...] = high
        other[...] = low


def arrived(core, got, low_blocks, high_blocks, sums, scale):
    peers = got.shape[0]
    _, width, size = low_blocks.shape
    return pl.pallas_call(
        functools.partial(arrived_kernel, scale),
        out_shape=(pltpu.VMEM((width, width // 2), F32),) * 2
        + (jax.ShapeDtypeStruct((peers,), jnp.int32),),
        in_specs=[SMEM, VMEM, VMEM, VMEM, VMEM],
        out_specs=(VMEM, VMEM, SMEM),
        compiler_params=params(8 + peers * size * width * 5 / MIB),
        name="arrived",
    )(core, got, low_blocks, high_blocks, sums)


def finish_kernel(
    ids, got, weight, base, nodes, out, near, ready, terms, held, last, count, came, left, end
):
    peers, size, width = near.shape
    half = width // 2

    def block(p):
        return pl.ds(pl.multiple_of(ids[p] * size, size), size)

    def read(p):
        return pltpu.make_async_copy(base.at[block(p)], near.at[p], came.at[p])

    def write(p):
        return pltpu.make_async_copy(ready.at[p], out.at[block(p)], left.at[p])

    def writes(p):
        return (ids[p] >= 0) & (last[ids[p] + 1] == p)

    second = pltpu.make_async_copy(weight.at[pl.ds(width, width)], held, end)
    second.start()

    def clear(b):
        count[b] = 0

    loop(last.shape[0], clear)

    def tally(p):
        last[ids[p] + 1] = p
        count[ids[p] + 1] += 1

    loop(peers, tally)

    def start(p):
        @pl.when(writes(p))
        def _():
            read(p).start()

    loop(peers, start)
    group = math.gcd(peers, 16)
    second.wait()

    def product(step):
        at = pl.ds(step * group, group)
        tile = jnp.concatenate([got[at, :size, :], got[at, size : 2 * size, :]], axis=2)
        tile = tile.reshape(group * size, width)
        terms[at] = dot_nt(tile, held[...]).reshape(group, size, width)

    loop(peers // group, product)

    def one(p):
        @pl.when(writes(p))
        def _():
            read(p).wait()

            @pl.when(count[ids[p] + 1] > 1)
            def _():
                def add(q, _):
                    @pl.when(ids[q] == ids[p])
                    def _():
                        near[p] += terms[q]

                    return 0

                lax.fori_loop(0, p, add, 0)

            ready[p] = (near[p] + terms[p]).astype(BF16)
            write(p).start()

    def drain(p):
        @pl.when(writes(p))
        def _():
            write(p).wait()

    loop(peers, one)
    loop(peers, drain)


def finish(ids, got, weight, base, nodes, size):
    peers = got.shape[0]
    width = base.shape[1]
    return pl.pallas_call(
        finish_kernel,
        out_shape=pltpu.HBM(nodes.shape, BF16),
        in_specs=[SMEM, VMEM, HBM, HBM, HBM],
        out_specs=HBM,
        scratch_shapes=[
            pltpu.VMEM((peers, size, width), F32),
            pltpu.VMEM((peers, size, width), BF16),
            pltpu.VMEM((peers, size, width), F32),
            pltpu.VMEM((width, width), BF16),
            pltpu.SMEM((nodes.shape[0] // size + 1,), jnp.int32),
            pltpu.SMEM((nodes.shape[0] // size + 1,), jnp.int32),
            pltpu.SemaphoreType.DMA((peers,)),
            pltpu.SemaphoreType.DMA((peers,)),
            pltpu.SemaphoreType.DMA(()),
        ],
        input_output_aliases={4: 0},
        compiler_params=params(6 + peers * size * width * 12 / MIB),
        cost_estimate=pl.CostEstimate(
            flops=2 * peers * size * width * width,
            bytes_accessed=peers * size * width * 8,
            transcendentals=0,
        ),
        name="finish",
    )(ids, got, *in_hbm(weight, base, nodes))


def swap(x, bit, peers):
    return lax.ppermute(x, "rows", [(i, i ^ bit) for i in range(peers)])


def widen(total, core, peers):
    there = swap(total, 1, peers)
    low, high = jnp.where(core == 0, total, there), jnp.where(core == 0, there, total)
    half = total.shape[0] // 2
    return [jnp.concatenate([x[:half], x[half:]], axis=1) for x in (low, high)]


def exchange(total, bit, peers):
    return total + swap(total.astype(BF16), bit, peers).astype(F32)


def local(
    node_features,
    preact,
    cotangent,
    weight,
    diag_tiles,
    edge_tiles,
    entry_rows,
    entry_owner,
    entry_cols,
):
    blocks, size, _ = diag_tiles.shape
    peers = lax.axis_size("rows")
    if peers & (peers - 1):
        raise ValueError("rows")
    core = lax.axis_index("rows") & 1
    which = core.reshape(1).astype(jnp.int32)
    scale = 1.0 / math.sqrt(peers * blocks * size)
    bits = [1 << i for i in range(1, peers.bit_length() - 1)]
    packed = pack(
        preact, cotangent, edge_tiles, entry_rows, entry_owner.reshape(-1), entry_cols, peers
    )
    got = lax.all_to_all(packed, "rows", split_axis=0, concat_axis=0, tiled=True)

    mine, other = first_sum(scale, which, node_features, preact, cotangent)
    first = mine + swap(other, 1, peers)
    arrays = (node_features, preact, cotangent, diag_tiles, weight)
    base, nodes, low_blocks, sums = local_work(scale, *arrays)
    for bit in bits[:-1]:
        first = exchange(first, bit, peers)
        if bit == 2:
            first, sums = lax.optimization_barrier((first, sums))
    base, nodes, high_blocks, sums = local_work(scale, *arrays, sums, base, nodes)
    sent = first.astype(BF16)
    first, sent, sums = lax.optimization_barrier((first, sent, sums))

    sent, got = lax.optimization_barrier((sent, got))
    mine, other, ids = arrived(which, got, low_blocks, high_blocks, sums, scale)
    second = mine + swap(other, 1, peers)
    first = first + swap(sent, bits[-1], peers).astype(F32)
    for bit in bits[:-1]:
        second = exchange(second, bit, peers)
    tied, second = lax.optimization_barrier((ids, second))
    nodes = finish(tied, got, weight, base, nodes, size)
    for bit in bits[-1:]:
        second = exchange(second, bit, peers)
    second, nodes = lax.optimization_barrier((second, nodes))
    rows = widen(first, core, peers) + widen(second, core, peers)
    return nodes, jnp.concatenate(rows, axis=0)


def solution(mesh):
    in_specs = (
        P(("parts", "rows"), None),
        P(("parts", "rows"), None),
        P(("parts", "rows"), None),
        P(),
        P(("parts", "rows"), None, None),
        P(("parts", "rows"), None, None),
        P(("parts", "rows")),
        P(("parts", "rows"), None),
        P(("parts", "rows")),
    )
    out_specs = (P(("parts", "rows"), None), P("parts", None))
    return jax.shard_map(local, mesh=mesh, in_specs=in_specs, out_specs=out_specs, check_vma=False)
```

```python
import functools
import math

import jax
import jax.numpy as jnp
from jax import lax
from jax.experimental import pallas as pl
from jax.experimental.pallas import tpu as pltpu
from jax.sharding import PartitionSpec as P

F32 = jnp.float32
BF16 = jnp.bfloat16
MIB = 1024 * 1024
TAG = 16
PACK_GROUP = 4
LOCAL_MIB = 58

VMEM = pl.BlockSpec(memory_space=pltpu.VMEM)
SMEM = pl.BlockSpec(memory_space=pltpu.SMEM)
HBM = pl.BlockSpec(memory_space=pltpu.HBM)


def in_hbm(*arrays):
    return [pltpu.with_memory_space_constraint(x, pltpu.HBM) for x in arrays]


def params(mib):
    return pltpu.CompilerParams(vmem_limit_bytes=int(mib * MIB))


def loop(count, body):
    lax.fori_loop(0, count, lambda i, _: (body(i), 0)[1], 0, unroll=count <= 16)


def dot_tn(a, b):
    return lax.dot_general(a, b, (((0,), (0,)), ((), ())), preferred_element_type=F32)


def dot_nt(a, b):
    return lax.dot_general(a, b, (((1,), (1,)), ((), ())), preferred_element_type=F32)


def pack_kernel(
    rows, owner, cols, preact, cotangent, tiles, out,
    rows_ref, owner_ref, cols_ref, held, pre, cot, ready, blank, used, sems, late, left,
):
    remote, size, width = pre.shape
    peers = out.shape[0]
    half = width // 2
    lists = [
        pltpu.make_async_copy(source, target, late.at[i])
        for i, (source, target) in enumerate(
            ((rows, rows_ref), (owner, owner_ref), (cols, cols_ref), (tiles, held))
        )
    ]
    for copy in lists:
        copy.start()
    blank[...] = jnp.zeros_like(blank)

    def unused(p):
        used[p] = 0

    loop(peers, unused)
    lists[0].wait()

    def fetch(k):
        block = pl.ds(pl.multiple_of(rows_ref[k] * size, size), size)
        return (
            pltpu.make_async_copy(preact.at[block], pre.at[k], sems.at[0, k]),
            pltpu.make_async_copy(cotangent.at[block], cot.at[k], sems.at[1, k]),
        )

    def start(k):
        for copy in fetch(k):
            copy.start()

    loop(remote, start)
    for copy in lists[1:]:
        copy.wait()

    def turn(k):
        held[k] = held[k].T

    loop(remote, turn)

    def mark(k):
        used[owner_ref[k]] = 1

    loop(remote, mark)

    def clear(p):
        return pltpu.make_async_copy(blank, out.at[p], left.at[p])

    def send(k):
        return pltpu.make_async_copy(ready.at[k], out.at[owner_ref[k]], left.at[peers + k])

    def start_clear(p):
        @pl.when(used[p] == 0)
        def _():
            clear(p).start()

    loop(peers, start_clear)

    def product(k):
        grad = jnp.where(pre[k] > 0, cot[k], jnp.zeros_like(cot[k]))
        term = jnp.dot(held[k], grad, preferred_element_type=F32).astype(BF16)
        ready[k, 0:size, :] = term[:, :half]
        ready[k, size : 2 * size, :] = term[:, half:]
        tag = (cols_ref[k] + 1).astype(F32)
        ready[k, 2 * size :, :] = jnp.full((TAG, half), tag, F32).astype(BF16)

    group = math.gcd(remote, PACK_GROUP)

    def batch(step):
        for k in range(group):
            for copy in fetch(step * group + k):
                copy.wait()
        for k in range(group):
            product(step * group + k)
        for k in range(group):
            send(step * group + k).start()

    loop(remote // group, batch)

    def end_clear(p):
        @pl.when(used[p] == 0)
        def _():
            clear(p).wait()

    loop(peers, end_clear)
    loop(remote, lambda k: send(k).wait())


def pack(preact, cotangent, tiles, rows, owner, cols, peers):
    remote, size, _ = tiles.shape
    width = preact.shape[1]
    return pl.pallas_call(
        pack_kernel,
        out_shape=jax.ShapeDtypeStruct((peers, 2 * size + TAG, width // 2), BF16),
        in_specs=[HBM] * 6,
        out_specs=HBM,
        scratch_shapes=[
            pltpu.SMEM((remote,), jnp.int32),
            pltpu.SMEM((remote,), jnp.int32),
            pltpu.SMEM((remote,), jnp.int32),
            pltpu.VMEM(tiles.shape, BF16),
            pltpu.VMEM((remote, size, width), BF16),
            pltpu.VMEM((remote, size, width), BF16),
            pltpu.VMEM((remote, 2 * size + TAG, width // 2), BF16),
            pltpu.VMEM((2 * size + TAG, width // 2), BF16),
            pltpu.SMEM((peers,), jnp.int32),
            pltpu.SemaphoreType.DMA((2, remote)),
            pltpu.SemaphoreType.DMA((4,)),
            pltpu.SemaphoreType.DMA((peers + remote,)),
        ],
        compiler_params=params(60),
        name="pack",
    )(*in_hbm(rows, owner, cols, preact, cotangent, tiles))


def fold(x):
    half = x.shape[1] // 2
    return jnp.concatenate([x[:, :half], x[:, half:]], axis=0)


def unfold(x):
    half = x.shape[0] // 2
    return jnp.concatenate([x[:half], x[half:]], axis=1)


def two_terms(x):
    high = x.astype(BF16)
    return high, (x - high.astype(F32)).astype(BF16)


def first_kernel(group, scale, core_ref, feat, preact, cotangent, mine, other, x, pre, cot, total, came):
    width = feat.shape[1]
    span = feat.shape[0] // group

    def arrive(i):
        at = pl.ds(pl.multiple_of(i * span, span), span)
        return (
            pltpu.make_async_copy(feat.at[at], x.at[at], came.at[0, i]),
            pltpu.make_async_copy(preact.at[at], pre.at[at], came.at[1, i]),
            pltpu.make_async_copy(cotangent.at[at], cot.at[at], came.at[2, i]),
        )

    def start(i):
        for copy in arrive(i):
            copy.start()

    loop(group, start)
    total[...] = jnp.zeros_like(total)

    def step(i, _):
        at = pl.ds(pl.multiple_of(i * span, span), span)
        for copy in arrive(i):
            copy.wait()
        grad = jnp.where(pre[at] > 0, cot[at], jnp.zeros((span, width), BF16))
        total[...] += dot_tn(x[at], grad)
        return 0

    lax.fori_loop(0, group, step, 0)
    half = width // 2
    low = fold(total[:half] * scale)
    high = fold(total[half:] * scale)

    @pl.when(core_ref[0] == 0)
    def _():
        mine[...] = low
        other[...] = high

    @pl.when(core_ref[0] != 0)
    def _():
        mine[...] = high
        other[...] = low


def first_sum(scale, core, feat, preact, cotangent):
    nodes, width = feat.shape
    group = 8
    return pl.pallas_call(
        functools.partial(first_kernel, group, scale),
        out_shape=(pltpu.VMEM((width, width // 2), F32),) * 2,
        in_specs=[SMEM, HBM, HBM, HBM],
        out_specs=(VMEM, VMEM),
        scratch_shapes=[
            pltpu.VMEM((nodes, width), BF16),
            pltpu.VMEM((nodes, width), BF16),
            pltpu.VMEM((nodes, width), BF16),
            pltpu.VMEM((width, width), F32),
            pltpu.SemaphoreType.DMA((3, group)),
        ],
        compiler_params=params(60),
        cost_estimate=pl.CostEstimate(
            flops=2 * nodes * width * width,
            bytes_accessed=nodes * width * 6,
            transcendentals=0,
        ),
        name="first_sum",
    )(core, *in_hbm(feat, preact, cotangent))


def local_kernel(group, part, scale, feat, preact, cotangent, diag, weight, *refs):
    base, nodes, turned, sums, x, pre, cot, tiles, full, rounded, total, came, left = refs[3 * part :]
    width = feat.shape[1]
    size = diag.shape[1]
    span = group * size
    steps = x.shape[0] // span
    origin = part * steps

    def here(i):
        return pl.ds(pl.multiple_of(i * span, span), span)

    def there(i):
        return here(origin + i)

    def arrive(i):
        some, same = pl.ds((origin + i) * group, group), pl.ds(i * group, group)
        return (
            pltpu.make_async_copy(preact.at[there(i)], pre.at[here(i)], came.at[0, i]),
            pltpu.make_async_copy(cotangent.at[there(i)], cot.at[here(i)], came.at[1, i]),
            pltpu.make_async_copy(diag.at[some], tiles.at[same], came.at[2, i]),
            pltpu.make_async_copy(feat.at[there(i)], x.at[here(i)], came.at[3, i]),
        )

    def leave(i):
        return (
            pltpu.make_async_copy(full.at[here(i)], base.at[there(i)], left.at[0, i]),
            pltpu.make_async_copy(rounded.at[here(i)], nodes.at[there(i)], left.at[1, i]),
        )

    def start(i):
        for copy in arrive(i):
            copy.start()

    loop(steps, start)
    total[...] = refs[0][...] if part else jnp.zeros_like(total)

    def step(i):
        at = here(i)
        for copy in arrive(i):
            copy.wait()
        grad = jnp.where(pre[at] > 0, cot[at], jnp.zeros((span, width), BF16))
        parts = [
            dot_tn(tiles[i * group + b], grad[b * size : (b + 1) * size]) for b in range(group)
        ]
        high, low = two_terms(jnp.concatenate(parts, axis=0))
        w_first, w_second = weight[:width], weight[width:]
        own = dot_nt(grad, w_first) + (dot_nt(high, w_second) + dot_nt(low, w_second))
        full[at] = own
        rounded[at] = own.astype(BF16)
        columns = x[at].T
        for b in range(group):
            turned[i * group + b] = columns[:, b * size : (b + 1) * size]
        for copy in leave(i):
            copy.start()
        total[...] += jnp.dot(columns, high, preferred_element_type=F32) + jnp.dot(
            columns, low, preferred_element_type=F32
        )

    lax.fori_loop(0, steps, lambda i, _: (step(i), 0)[1], 0)
    sums[...] = total[...] * scale if part else total[...]

    def drain(i):
        for copy in leave(i):
            copy.wait()

    loop(steps, drain)


def local_work(scale, feat, preact, cotangent, diag, weight, *state):
    part = 1 if state else 0
    rows, width = feat.shape
    blocks, size, _ = diag.shape
    group = math.gcd(blocks // 2, 4)
    steps = blocks // 2 // group
    return pl.pallas_call(
        functools.partial(local_kernel, group, part, scale),
        out_shape=(
            pltpu.HBM((rows, width), F32),
            pltpu.HBM((rows, width), BF16),
            pltpu.VMEM((blocks // 2, width, size), BF16),
            pltpu.VMEM((width, width), F32),
        ),
        in_specs=[HBM, HBM, HBM, HBM, VMEM] + [VMEM, HBM, HBM][: len(state)],
        out_specs=(HBM, HBM, VMEM, VMEM),
        scratch_shapes=[
            pltpu.VMEM((rows // 2, width), BF16),
            pltpu.VMEM((rows // 2, width), BF16),
            pltpu.VMEM((rows // 2, width), BF16),
            pltpu.VMEM((blocks // 2, size, size), BF16),
            pltpu.VMEM((rows // 2, width), F32),
            pltpu.VMEM((rows // 2, width), BF16),
            pltpu.VMEM((width, width), F32),
            pltpu.SemaphoreType.DMA((4, steps)),
            pltpu.SemaphoreType.DMA((2, steps)),
        ],
        input_output_aliases={6: 0, 7: 1} if part else {},
        compiler_params=params(LOCAL_MIB),
        cost_estimate=pl.CostEstimate(
            flops=rows * width * (size + 5 * width),
            bytes_accessed=rows * width * 7 + blocks * size * size,
            transcendentals=0,
        ),
        name="local_work",
    )(*in_hbm(feat, preact, cotangent, diag), weight, *state[:1], *in_hbm(*state[1:]))


def arrived_kernel(scale, core_ref, got, low_blocks, high_blocks, sums, mine, other, ids):
    peers = got.shape[0]
    half, width, size = low_blocks.shape
    group = math.gcd(peers, 16)

    def mark(p):
        ids[p] = jnp.max(got[p, 2 * size :, :].astype(F32)).astype(jnp.int32) - 1

    loop(peers, mark)

    def block(p):
        at = ids[p]
        low = low_blocks[jnp.clip(at, 0, half - 1)]
        high = high_blocks[jnp.maximum(at - half, 0)]
        return jnp.where(at < half, low, high)

    def term(step, total):
        for q in range(0, group, 2):
            pair = (step * group + q, step * group + q + 1)
            left = jnp.concatenate([block(p) for p in pair], axis=1)
            right = jnp.concatenate([unfold(got[p, : 2 * size, :]) for p in pair], axis=0)
            total = total + jnp.dot(left, right, preferred_element_type=F32)
        return total

    total = jnp.zeros((width, width), F32)
    total = lax.fori_loop(0, peers // group, term, total, unroll=peers == group)
    total = total * scale + sums[...]
    low, high = fold(total[: width // 2]), fold(total[width // 2 :])

    @pl.when(core_ref[0] == 0)
    def _():
        mine[...] = low
        other[...] = high

    @pl.when(core_ref[0] != 0)
    def _():
        mine[...] = high
        other[...] = low


def arrived(core, got, low_blocks, high_blocks, sums, scale):
    peers = got.shape[0]
    _, width, size = low_blocks.shape
    return pl.pallas_call(
        functools.partial(arrived_kernel, scale),
        out_shape=(pltpu.VMEM((width, width // 2), F32),) * 2
        + (jax.ShapeDtypeStruct((peers,), jnp.int32),),
        in_specs=[SMEM, VMEM, VMEM, VMEM, VMEM],
        out_specs=(VMEM, VMEM, SMEM),
        compiler_params=params(8 + peers * size * width * 5 / MIB),
        name="arrived",
    )(core, got, low_blocks, high_blocks, sums)


def finish_kernel(
    ids, got, weight, base, nodes, out, near, ready, terms, held, last, count, came, left, end
):
    peers, size, width = near.shape
    half = width // 2

    def block(p):
        return pl.ds(pl.multiple_of(ids[p] * size, size), size)

    def read(p):
        return pltpu.make_async_copy(base.at[block(p)], near.at[p], came.at[p])

    def write(p):
        return pltpu.make_async_copy(ready.at[p], out.at[block(p)], left.at[p])

    def writes(p):
        return (ids[p] >= 0) & (last[ids[p] + 1] == p)

    second = pltpu.make_async_copy(weight.at[pl.ds(width, width)], held, end)
    second.start()

    def clear(b):
        count[b] = 0

    loop(last.shape[0], clear)

    def tally(p):
        last[ids[p] + 1] = p
        count[ids[p] + 1] += 1

    loop(peers, tally)

    def start(p):
        @pl.when(writes(p))
        def _():
            read(p).start()

    loop(peers, start)
    group = math.gcd(peers, 16)
    second.wait()

    def product(step):
        at = pl.ds(step * group, group)
        tile = jnp.concatenate([got[at, :size, :], got[at, size : 2 * size, :]], axis=2)
        tile = tile.reshape(group * size, width)
        terms[at] = dot_nt(tile, held[...]).reshape(group, size, width)

    loop(peers // group, product)

    def one(p):
        @pl.when(writes(p))
        def _():
            read(p).wait()

            @pl.when(count[ids[p] + 1] > 1)
            def _():
                def add(q, _):
                    @pl.when(ids[q] == ids[p])
                    def _():
                        near[p] += terms[q]

                    return 0

                lax.fori_loop(0, p, add, 0)

            ready[p] = (near[p] + terms[p]).astype(BF16)
            write(p).start()

    def drain(p):
        @pl.when(writes(p))
        def _():
            write(p).wait()

    loop(peers, one)
    loop(peers, drain)


def finish(ids, got, weight, base, nodes, size):
    peers = got.shape[0]
    width = base.shape[1]
    return pl.pallas_call(
        finish_kernel,
        out_shape=pltpu.HBM(nodes.shape, BF16),
        in_specs=[SMEM, VMEM, HBM, HBM, HBM],
        out_specs=HBM,
        scratch_shapes=[
            pltpu.VMEM((peers, size, width), F32),
            pltpu.VMEM((peers, size, width), BF16),
            pltpu.VMEM((peers, size, width), F32),
            pltpu.VMEM((width, width), BF16),
            pltpu.SMEM((nodes.shape[0] // size + 1,), jnp.int32),
            pltpu.SMEM((nodes.shape[0] // size + 1,), jnp.int32),
            pltpu.SemaphoreType.DMA((peers,)),
            pltpu.SemaphoreType.DMA((peers,)),
            pltpu.SemaphoreType.DMA(()),
        ],
        input_output_aliases={4: 0},
        compiler_params=params(6 + peers * size * width * 12 / MIB),
        cost_estimate=pl.CostEstimate(
            flops=2 * peers * size * width * width,
            bytes_accessed=peers * size * width * 8,
            transcendentals=0,
        ),
        name="finish",
    )(ids, got, *in_hbm(weight, base, nodes))


def swap(x, bit, peers):
    return lax.ppermute(x, "rows", [(i, i ^ bit) for i in range(peers)])


def widen(total, core, peers):
    there = swap(total, 1, peers)
    low, high = jnp.where(core == 0, total, there), jnp.where(core == 0, there, total)
    half = total.shape[0] // 2
    return [jnp.concatenate([x[:half], x[half:]], axis=1) for x in (low, high)]


def exchange(total, bit, peers):
    return total + swap(total.astype(BF16), bit, peers).astype(F32)


def local(
    node_features,
    preact,
    cotangent,
    weight,
    diag_tiles,
    edge_tiles,
    entry_rows,
    entry_owner,
    entry_cols,
):
    blocks, size, _ = diag_tiles.shape
    peers = lax.axis_size("rows")
    if peers & (peers - 1):
        raise ValueError("rows")
    core = lax.axis_index("rows") & 1
    which = core.reshape(1).astype(jnp.int32)
    scale = 1.0 / math.sqrt(peers * blocks * size)
    bits = [1 << i for i in range(1, peers.bit_length() - 1)]
    packed = pack(
        preact, cotangent, edge_tiles, entry_rows, entry_owner.reshape(-1), entry_cols, peers
    )
    got = lax.all_to_all(packed, "rows", split_axis=0, concat_axis=0, tiled=True)

    mine, other = first_sum(scale, which, node_features, preact, cotangent)
    first = mine + swap(other, 1, peers)
    arrays = (node_features, preact, cotangent, diag_tiles, weight)
    base, nodes, low_blocks, sums = local_work(scale, *arrays)
    for bit in bits[:-1]:
        first = exchange(first, bit, peers)
        if bit == 2:
            first, sums = lax.optimization_barrier((first, sums))
    base, nodes, high_blocks, sums = local_work(scale, *arrays, sums, base, nodes)
    sent = first.astype(BF16)
    first, sent, sums = lax.optimization_barrier((first, sent, sums))

    sent, got = lax.optimization_barrier((sent, got))
    mine, other, ids = arrived(which, got, low_blocks, high_blocks, sums, scale)
    second = mine + swap(other, 1, peers)
    first = first + swap(sent, bits[-1], peers).astype(F32)
    for bit in bits[:-1]:
        second = exchange(second, bit, peers)
    tied, second = lax.optimization_barrier((ids, second))
    nodes = finish(tied, got, weight, base, nodes, size)
    for bit in bits[-1:]:
        second = exchange(second, bit, peers)
    second, nodes = lax.optimization_barrier((second, nodes))
    rows = widen(first, core, peers) + widen(second, core, peers)
    return nodes, jnp.concatenate(rows, axis=0)


def solution(mesh):
    in_specs = (
        P(("parts", "rows"), None),
        P(("parts", "rows"), None),
        P(("parts", "rows"), None),
        P(),
        P(("parts", "rows"), None, None),
        P(("parts", "rows"), None, None),
        P(("parts", "rows")),
        P(("parts", "rows"), None),
        P(("parts", "rows")),
    )
    out_specs = (P(("parts", "rows"), None), P("parts", None))
    return jax.shard_map(local, mesh=mesh, in_specs=in_specs, out_specs=out_specs, check_vma=False)
```

```python
import functools
import math

import jax
import jax.numpy as jnp
from jax import lax
from jax.experimental import pallas as pl
from jax.experimental.pallas import tpu as pltpu
from jax.sharding import PartitionSpec as P

F32 = jnp.float32
BF16 = jnp.bfloat16
MIB = 1024 * 1024
TAG = 16
PACK_GROUP = 4
LOCAL_MIB = 58

VMEM = pl.BlockSpec(memory_space=pltpu.VMEM)
SMEM = pl.BlockSpec(memory_space=pltpu.SMEM)
HBM = pl.BlockSpec(memory_space=pltpu.HBM)


def in_hbm(*arrays):
    return [pltpu.with_memory_space_constraint(x, pltpu.HBM) for x in arrays]


def params(mib):
    return pltpu.CompilerParams(vmem_limit_bytes=int(mib * MIB))


def loop(count, body):
    lax.fori_loop(0, count, lambda i, _: (body(i), 0)[1], 0, unroll=count <= 16)


def dot_tn(a, b):
    return lax.dot_general(a, b, (((0,), (0,)), ((), ())), preferred_element_type=F32)


def dot_nt(a, b):
    return lax.dot_general(a, b, (((1,), (1,)), ((), ())), preferred_element_type=F32)


def pack_kernel(
    rows, owner, cols, preact, cotangent, tiles, out,
    rows_ref, owner_ref, cols_ref, held, pre, cot, ready, blank, used, sems, late, left,
):
    remote, size, width = pre.shape
    peers = out.shape[0]
    half = width // 2
    lists = [
        pltpu.make_async_copy(source, target, late.at[i])
        for i, (source, target) in enumerate(
            ((rows, rows_ref), (owner, owner_ref), (cols, cols_ref), (tiles, held))
        )
    ]
    for copy in lists:
        copy.start()
    blank[...] = jnp.zeros_like(blank)

    def unused(p):
        used[p] = 0

    loop(peers, unused)
    lists[0].wait()

    def fetch(k):
        block = pl.ds(pl.multiple_of(rows_ref[k] * size, size), size)
        return (
            pltpu.make_async_copy(preact.at[block], pre.at[k], sems.at[0, k]),
            pltpu.make_async_copy(cotangent.at[block], cot.at[k], sems.at[1, k]),
        )

    def start(k):
        for copy in fetch(k):
            copy.start()

    loop(remote, start)
    for copy in lists[1:]:
        copy.wait()

    def turn(k):
        held[k] = held[k].T

    loop(remote, turn)

    def mark(k):
        used[owner_ref[k]] = 1

    loop(remote, mark)

    def clear(p):
        return pltpu.make_async_copy(blank, out.at[p], left.at[p])

    def send(k):
        return pltpu.make_async_copy(ready.at[k], out.at[owner_ref[k]], left.at[peers + k])

    def start_clear(p):
        @pl.when(used[p] == 0)
        def _():
            clear(p).start()

    loop(peers, start_clear)

    def product(k):
        grad = jnp.where(pre[k] > 0, cot[k], jnp.zeros_like(cot[k]))
        term = jnp.dot(held[k], grad, preferred_element_type=F32).astype(BF16)
        ready[k, 0:size, :] = term[:, :half]
        ready[k, size : 2 * size, :] = term[:, half:]
        tag = (cols_ref[k] + 1).astype(F32)
        ready[k, 2 * size :, :] = jnp.full((TAG, half), tag, F32).astype(BF16)

    group = math.gcd(remote, PACK_GROUP)

    def batch(step):
        for k in range(group):
            for copy in fetch(step * group + k):
                copy.wait()
        for k in range(group):
            product(step * group + k)
        for k in range(group):
            send(step * group + k).start()

    loop(remote // group, batch)

    def end_clear(p):
        @pl.when(used[p] == 0)
        def _():
            clear(p).wait()

    loop(peers, end_clear)
    loop(remote, lambda k: send(k).wait())


def pack(preact, cotangent, tiles, rows, owner, cols, peers):
    remote, size, _ = tiles.shape
    width = preact.shape[1]
    return pl.pallas_call(
        pack_kernel,
        out_shape=jax.ShapeDtypeStruct((peers, 2 * size + TAG, width // 2), BF16),
        in_specs=[HBM] * 6,
        out_specs=HBM,
        scratch_shapes=[
            pltpu.SMEM((remote,), jnp.int32),
            pltpu.SMEM((remote,), jnp.int32),
            pltpu.SMEM((remote,), jnp.int32),
            pltpu.VMEM(tiles.shape, BF16),
            pltpu.VMEM((remote, size, width), BF16),
            pltpu.VMEM((remote, size, width), BF16),
            pltpu.VMEM((remote, 2 * size + TAG, width // 2), BF16),
            pltpu.VMEM((2 * size + TAG, width // 2), BF16),
            pltpu.SMEM((peers,), jnp.int32),
            pltpu.SemaphoreType.DMA((2, remote)),
            pltpu.SemaphoreType.DMA((4,)),
            pltpu.SemaphoreType.DMA((peers + remote,)),
        ],
        compiler_params=params(60),
        name="pack",
    )(*in_hbm(rows, owner, cols, preact, cotangent, tiles))


def fold(x):
    half = x.shape[1] // 2
    return jnp.concatenate([x[:, :half], x[:, half:]], axis=0)


def unfold(x):
    half = x.shape[0] // 2
    return jnp.concatenate([x[:half], x[half:]], axis=1)


def two_terms(x):
    high = x.astype(BF16)
    return high, (x - high.astype(F32)).astype(BF16)


def first_kernel(group, scale, core_ref, feat, preact, cotangent, mine, other, x, pre, cot, total, came):
    width = feat.shape[1]
    span = feat.shape[0] // group

    def arrive(i):
        at = pl.ds(pl.multiple_of(i * span, span), span)
        return (
            pltpu.make_async_copy(feat.at[at], x.at[at], came.at[0, i]),
            pltpu.make_async_copy(preact.at[at], pre.at[at], came.at[1, i]),
            pltpu.make_async_copy(cotangent.at[at], cot.at[at], came.at[2, i]),
        )

    def start(i):
        for copy in arrive(i):
            copy.start()

    loop(group, start)
    total[...] = jnp.zeros_like(total)

    def step(i, _):
        at = pl.ds(pl.multiple_of(i * span, span), span)
        for copy in arrive(i):
            copy.wait()
        grad = jnp.where(pre[at] > 0, cot[at], jnp.zeros((span, width), BF16))
        total[...] += dot_tn(x[at], grad)
        return 0

    lax.fori_loop(0, group, step, 0)
    half = width // 2
    low = fold(total[:half] * scale)
    high = fold(total[half:] * scale)

    @pl.when(core_ref[0] == 0)
    def _():
        mine[...] = low
        other[...] = high

    @pl.when(core_ref[0] != 0)
    def _():
        mine[...] = high
        other[...] = low


def first_sum(scale, core, feat, preact, cotangent):
    nodes, width = feat.shape
    group = 8
    return pl.pallas_call(
        functools.partial(first_kernel, group, scale),
        out_shape=(pltpu.VMEM((width, width // 2), F32),) * 2,
        in_specs=[SMEM, HBM, HBM, HBM],
        out_specs=(VMEM, VMEM),
        scratch_shapes=[
            pltpu.VMEM((nodes, width), BF16),
            pltpu.VMEM((nodes, width), BF16),
            pltpu.VMEM((nodes, width), BF16),
            pltpu.VMEM((width, width), F32),
            pltpu.SemaphoreType.DMA((3, group)),
        ],
        compiler_params=params(60),
        cost_estimate=pl.CostEstimate(
            flops=2 * nodes * width * width,
            bytes_accessed=nodes * width * 6,
            transcendentals=0,
        ),
        name="first_sum",
    )(core, *in_hbm(feat, preact, cotangent))


def local_kernel(group, part, scale, feat, preact, cotangent, diag, weight, *refs):
    base, nodes, turned, sums, x, pre, cot, tiles, full, rounded, total, came, left = refs[3 * part :]
    width = feat.shape[1]
    size = diag.shape[1]
    span = group * size
    steps = x.shape[0] // span
    origin = part * steps

    def here(i):
        return pl.ds(pl.multiple_of(i * span, span), span)

    def there(i):
        return here(origin + i)

    def arrive(i):
        some, same = pl.ds((origin + i) * group, group), pl.ds(i * group, group)
        return (
            pltpu.make_async_copy(preact.at[there(i)], pre.at[here(i)], came.at[0, i]),
            pltpu.make_async_copy(cotangent.at[there(i)], cot.at[here(i)], came.at[1, i]),
            pltpu.make_async_copy(diag.at[some], tiles.at[same], came.at[2, i]),
            pltpu.make_async_copy(feat.at[there(i)], x.at[here(i)], came.at[3, i]),
        )

    def leave(i):
        return (
            pltpu.make_async_copy(full.at[here(i)], base.at[there(i)], left.at[0, i]),
            pltpu.make_async_copy(rounded.at[here(i)], nodes.at[there(i)], left.at[1, i]),
        )

    def start(i):
        for copy in arrive(i):
            copy.start()

    loop(steps, start)
    total[...] = refs[0][...] if part else jnp.zeros_like(total)

    def step(i):
        at = here(i)
        for copy in arrive(i):
            copy.wait()
        grad = jnp.where(pre[at] > 0, cot[at], jnp.zeros((span, width), BF16))
        parts = [
            dot_tn(tiles[i * group + b], grad[b * size : (b + 1) * size]) for b in range(group)
        ]
        high, low = two_terms(jnp.concatenate(parts, axis=0))
        w_first, w_second = weight[:width], weight[width:]
        own = dot_nt(grad, w_first) + (dot_nt(high, w_second) + dot_nt(low, w_second))
        full[at] = own
        rounded[at] = own.astype(BF16)
        columns = x[at].T
        for b in range(group):
            turned[i * group + b] = columns[:, b * size : (b + 1) * size]
        for copy in leave(i):
            copy.start()
        total[...] += jnp.dot(columns, high, preferred_element_type=F32) + jnp.dot(
            columns, low, preferred_element_type=F32
        )

    lax.fori_loop(0, steps, lambda i, _: (step(i), 0)[1], 0)
    sums[...] = total[...] * scale if part else total[...]

    def drain(i):
        for copy in leave(i):
            copy.wait()

    loop(steps, drain)


def local_work(scale, feat, preact, cotangent, diag, weight, *state):
    part = 1 if state else 0
    rows, width = feat.shape
    blocks, size, _ = diag.shape
    group = math.gcd(blocks // 2, 4)
    steps = blocks // 2 // group
    return pl.pallas_call(
        functools.partial(local_kernel, group, part, scale),
        out_shape=(
            pltpu.HBM((rows, width), F32),
            pltpu.HBM((rows, width), BF16),
            pltpu.VMEM((blocks // 2, width, size), BF16),
            pltpu.VMEM((width, width), F32),
        ),
        in_specs=[HBM, HBM, HBM, HBM, VMEM] + [VMEM, HBM, HBM][: len(state)],
        out_specs=(HBM, HBM, VMEM, VMEM),
        scratch_shapes=[
            pltpu.VMEM((rows // 2, width), BF16),
            pltpu.VMEM((rows // 2, width), BF16),
            pltpu.VMEM((rows // 2, width), BF16),
            pltpu.VMEM((blocks // 2, size, size), BF16),
            pltpu.VMEM((rows // 2, width), F32),
            pltpu.VMEM((rows // 2, width), BF16),
            pltpu.VMEM((width, width), F32),
            pltpu.SemaphoreType.DMA((4, steps)),
            pltpu.SemaphoreType.DMA((2, steps)),
        ],
        input_output_aliases={6: 0, 7: 1} if part else {},
        compiler_params=params(LOCAL_MIB),
        cost_estimate=pl.CostEstimate(
            flops=rows * width * (size + 5 * width),
            bytes_accessed=rows * width * 7 + blocks * size * size,
            transcendentals=0,
        ),
        name="local_work",
    )(*in_hbm(feat, preact, cotangent, diag), weight, *state[:1], *in_hbm(*state[1:]))


def half_sum(scale, row, ids, got, low_blocks, high_blocks, sums):
    peers = got.shape[0]
    half, width, size = low_blocks.shape
    group = math.gcd(peers, 16)
    wide = math.gcd(group, 4)
    rows = pl.ds(pl.multiple_of(row, width // 2), width // 2)

    def block(p):
        at = ids[p]
        low = low_blocks[jnp.clip(at, 0, half - 1), rows, :]
        high = high_blocks[jnp.maximum(at - half, 0), rows, :]
        return jnp.where(at < half, low, high)

    def term(step, total):
        for q in range(0, group, wide):
            pair = [step * group + q + k for k in range(wide)]
            left = jnp.concatenate([block(p) for p in pair], axis=1)
            right = jnp.concatenate([unfold(got[p, : 2 * size, :]) for p in pair], axis=0)
            total = total + jnp.dot(left, right, preferred_element_type=F32)
        return total

    total = jnp.zeros((width // 2, width), F32)
    total = lax.fori_loop(0, peers // group, term, total, unroll=peers == group)
    return fold(total * scale + sums[rows, :])


def theirs_kernel(scale, core_ref, got, low_blocks, high_blocks, sums, other, ids):
    size = low_blocks.shape[2]

    def mark(p):
        ids[p] = jnp.max(got[p, 2 * size :, :].astype(F32)).astype(jnp.int32) - 1

    loop(got.shape[0], mark)
    row = (1 - core_ref[0]) * (sums.shape[0] // 2)
    other[...] = half_sum(scale, row, ids, got, low_blocks, high_blocks, sums)


def ours_kernel(scale, core_ref, ids, got, low_blocks, high_blocks, sums, mine):
    row = core_ref[0] * (sums.shape[0] // 2)
    mine[...] = half_sum(scale, row, ids, got, low_blocks, high_blocks, sums)


def arrived(core, got, low_blocks, high_blocks, sums, scale):
    peers = got.shape[0]
    _, width, size = low_blocks.shape
    return pl.pallas_call(
        functools.partial(theirs_kernel, scale),
        out_shape=(
            pltpu.VMEM((width, width // 2), F32),
            jax.ShapeDtypeStruct((peers,), jnp.int32),
        ),
        in_specs=[SMEM, VMEM, VMEM, VMEM, VMEM],
        out_specs=(VMEM, SMEM),
        compiler_params=params(8 + peers * size * width * 5 / MIB),
        name="arrived",
    )(core, got, low_blocks, high_blocks, sums)


def own_half(core, ids, got, low_blocks, high_blocks, sums, scale):
    peers = got.shape[0]
    _, width, size = low_blocks.shape
    return pl.pallas_call(
        functools.partial(ours_kernel, scale),
        out_shape=pltpu.VMEM((width, width // 2), F32),
        in_specs=[SMEM, SMEM, VMEM, VMEM, VMEM, VMEM],
        out_specs=VMEM,
        compiler_params=params(8 + peers * size * width * 5 / MIB),
        name="own_half",
    )(core, ids, got, low_blocks, high_blocks, sums)


def finish_kernel(
    ids, got, weight, base, nodes, out, near, ready, terms, last, count, came, left
):
    peers, size, width = near.shape
    half = width // 2

    def block(p):
        return pl.ds(pl.multiple_of(ids[p] * size, size), size)

    def read(p):
        return pltpu.make_async_copy(base.at[block(p)], near.at[p], came.at[p])

    def write(p):
        return pltpu.make_async_copy(ready.at[p], out.at[block(p)], left.at[p])

    def writes(p):
        return (ids[p] >= 0) & (last[ids[p] + 1] == p)

    def start(p):
        @pl.when(ids[p] >= 0)
        def _():
            read(p).start()

    loop(peers, start)

    def clear(b):
        count[b] = 0

    loop(last.shape[0], clear)

    def tally(p):
        last[ids[p] + 1] = p
        count[ids[p] + 1] += 1

    loop(peers, tally)

    group = math.gcd(peers, 16)

    def product(step):
        at = pl.ds(step * group, group)
        tile = jnp.concatenate([got[at, :size, :], got[at, size : 2 * size, :]], axis=2)
        tile = tile.reshape(group * size, width)
        terms[at] = dot_nt(tile, weight[...]).reshape(group, size, width)

    loop(peers // group, product)

    def one(p):
        @pl.when(ids[p] >= 0)
        def _():
            read(p).wait()

        @pl.when(writes(p))
        def _():
            @pl.when(count[ids[p] + 1] > 1)
            def _():
                def add(q, _):
                    @pl.when(ids[q] == ids[p])
                    def _():
                        near[p] += terms[q]

                    return 0

                lax.fori_loop(0, p, add, 0)

            ready[p] = (near[p] + terms[p]).astype(BF16)
            write(p).start()

    def drain(p):
        @pl.when(writes(p))
        def _():
            write(p).wait()

    loop(peers, one)
    loop(peers, drain)


def finish(ids, got, weight, base, nodes, size):
    peers = got.shape[0]
    width = base.shape[1]
    return pl.pallas_call(
        finish_kernel,
        out_shape=pltpu.HBM(nodes.shape, BF16),
        in_specs=[SMEM, VMEM, VMEM, HBM, HBM],
        out_specs=HBM,
        scratch_shapes=[
            pltpu.VMEM((peers, size, width), F32),
            pltpu.VMEM((peers, size, width), BF16),
            pltpu.VMEM((peers, size, width), F32),
            pltpu.SMEM((nodes.shape[0] // size + 1,), jnp.int32),
            pltpu.SMEM((nodes.shape[0] // size + 1,), jnp.int32),
            pltpu.SemaphoreType.DMA((peers,)),
            pltpu.SemaphoreType.DMA((peers,)),
        ],
        input_output_aliases={4: 0},
        compiler_params=params(6 + peers * size * width * 12 / MIB),
        cost_estimate=pl.CostEstimate(
            flops=2 * peers * size * width * width,
            bytes_accessed=peers * size * width * 8,
            transcendentals=0,
        ),
        name="finish",
    )(ids, got, weight[width:], *in_hbm(base, nodes))


def swap(x, bit, peers):
    return lax.ppermute(x, "rows", [(i, i ^ bit) for i in range(peers)])


def widen(total, core, peers):
    there = swap(total, 1, peers)
    low, high = jnp.where(core == 0, total, there), jnp.where(core == 0, there, total)
    half = total.shape[0] // 2
    return [jnp.concatenate([x[:half], x[half:]], axis=1) for x in (low, high)]


def exchange(total, bit, peers):
    return total + swap(total.astype(BF16), bit, peers).astype(F32)


def local(
    node_features,
    preact,
    cotangent,
    weight,
    diag_tiles,
    edge_tiles,
    entry_rows,
    entry_owner,
    entry_cols,
):
    blocks, size, _ = diag_tiles.shape
    peers = lax.axis_size("rows")
    if peers & (peers - 1):
        raise ValueError("rows")
    core = lax.axis_index("rows") & 1
    which = core.reshape(1).astype(jnp.int32)
    scale = 1.0 / math.sqrt(peers * blocks * size)
    bits = [1 << i for i in range(1, peers.bit_length() - 1)]
    packed = pack(
        preact, cotangent, edge_tiles, entry_rows, entry_owner.reshape(-1), entry_cols, peers
    )
    got = lax.all_to_all(packed, "rows", split_axis=0, concat_axis=0, tiled=True)

    mine, other = first_sum(scale, which, node_features, preact, cotangent)
    first = mine + swap(other, 1, peers)
    arrays = (node_features, preact, cotangent, diag_tiles, weight)
    base, nodes, low_blocks, sums = local_work(scale, *arrays)
    for bit in bits[:-1]:
        first = exchange(first, bit, peers)
        if bit == 2:
            first, sums = lax.optimization_barrier((first, sums))
    base, nodes, high_blocks, sums = local_work(scale, *arrays, sums, base, nodes)
    sent = first.astype(BF16)
    first, sent, sums = lax.optimization_barrier((first, sent, sums))

    sent, got = lax.optimization_barrier((sent, got))
    other, ids = arrived(which, got, low_blocks, high_blocks, sums, scale)
    mine = own_half(which, ids, got, low_blocks, high_blocks, sums, scale)
    second = mine + swap(other, 1, peers)
    first = first + swap(sent, bits[-1], peers).astype(F32)
    for bit in bits[:-1]:
        second = exchange(second, bit, peers)
    tied, second = lax.optimization_barrier((ids, second))
    nodes = finish(tied, got, weight, base, nodes, size)
    for bit in bits[-1:]:
        second = exchange(second, bit, peers)
    second, nodes = lax.optimization_barrier((second, nodes))
    rows = widen(first, core, peers) + widen(second, core, peers)
    return nodes, jnp.concatenate(rows, axis=0)


def solution(mesh):
    in_specs = (
        P(("parts", "rows"), None),
        P(("parts", "rows"), None),
        P(("parts", "rows"), None),
        P(),
        P(("parts", "rows"), None, None),
        P(("parts", "rows"), None, None),
        P(("parts", "rows")),
        P(("parts", "rows"), None),
        P(("parts", "rows")),
    )
    out_specs = (P(("parts", "rows"), None), P("parts", None))
    return jax.shard_map(local, mesh=mesh, in_specs=in_specs, out_specs=out_specs, check_vma=False)
```

```python
import functools
import math

import jax
import jax.numpy as jnp
from jax import lax
from jax.experimental import pallas as pl
from jax.experimental.pallas import tpu as pltpu
from jax.sharding import PartitionSpec as P

F32 = jnp.float32
BF16 = jnp.bfloat16
MIB = 1024 * 1024
TAG = 16
PACK_GROUP = 4
LOCAL_MIB = 58

VMEM = pl.BlockSpec(memory_space=pltpu.VMEM)
SMEM = pl.BlockSpec(memory_space=pltpu.SMEM)
HBM = pl.BlockSpec(memory_space=pltpu.HBM)


def in_hbm(*arrays):
    return [pltpu.with_memory_space_constraint(x, pltpu.HBM) for x in arrays]


def params(mib):
    return pltpu.CompilerParams(vmem_limit_bytes=int(mib * MIB))


def loop(count, body):
    lax.fori_loop(0, count, lambda i, _: (body(i), 0)[1], 0, unroll=count <= 16)


def dot_tn(a, b):
    return lax.dot_general(a, b, (((0,), (0,)), ((), ())), preferred_element_type=F32)


def dot_nt(a, b):
    return lax.dot_general(a, b, (((1,), (1,)), ((), ())), preferred_element_type=F32)


def pack_kernel(
    rows, owner, cols, preact, cotangent, tiles, out,
    rows_ref, owner_ref, cols_ref, held, pre, cot, ready, blank, used, sems, late, left,
):
    remote, size, width = pre.shape
    peers = out.shape[0]
    half = width // 2
    lists = [
        pltpu.make_async_copy(source, target, late.at[i])
        for i, (source, target) in enumerate(
            ((rows, rows_ref), (owner, owner_ref), (cols, cols_ref), (tiles, held))
        )
    ]
    for copy in lists:
        copy.start()
    blank[...] = jnp.zeros_like(blank)

    def unused(p):
        used[p] = 0

    loop(peers, unused)
    lists[0].wait()

    def fetch(k):
        block = pl.ds(pl.multiple_of(rows_ref[k] * size, size), size)
        return (
            pltpu.make_async_copy(preact.at[block], pre.at[k], sems.at[0, k]),
            pltpu.make_async_copy(cotangent.at[block], cot.at[k], sems.at[1, k]),
        )

    def start(k):
        for copy in fetch(k):
            copy.start()

    loop(remote, start)
    for copy in lists[1:]:
        copy.wait()

    def turn(k):
        held[k] = held[k].T

    loop(remote, turn)

    def mark(k):
        used[owner_ref[k]] = 1

    loop(remote, mark)

    def clear(p):
        return pltpu.make_async_copy(blank, out.at[p], left.at[p])

    def send(k):
        return pltpu.make_async_copy(ready.at[k], out.at[owner_ref[k]], left.at[peers + k])

    def start_clear(p):
        @pl.when(used[p] == 0)
        def _():
            clear(p).start()

    loop(peers, start_clear)

    def product(k):
        grad = jnp.where(pre[k] > 0, cot[k], jnp.zeros_like(cot[k]))
        term = jnp.dot(held[k], grad, preferred_element_type=F32).astype(BF16)
        ready[k, 0:size, :] = term[:, :half]
        ready[k, size : 2 * size, :] = term[:, half:]
        tag = (cols_ref[k] + 1).astype(F32)
        ready[k, 2 * size :, :] = jnp.full((TAG, half), tag, F32).astype(BF16)

    group = math.gcd(remote, PACK_GROUP)

    def batch(step):
        for k in range(group):
            for copy in fetch(step * group + k):
                copy.wait()
        for k in range(group):
            product(step * group + k)
        for k in range(group):
            send(step * group + k).start()

    loop(remote // group, batch)

    def end_clear(p):
        @pl.when(used[p] == 0)
        def _():
            clear(p).wait()

    loop(peers, end_clear)
    loop(remote, lambda k: send(k).wait())


def pack(preact, cotangent, tiles, rows, owner, cols, peers):
    remote, size, _ = tiles.shape
    width = preact.shape[1]
    return pl.pallas_call(
        pack_kernel,
        out_shape=jax.ShapeDtypeStruct((peers, 2 * size + TAG, width // 2), BF16),
        in_specs=[HBM] * 6,
        out_specs=HBM,
        scratch_shapes=[
            pltpu.SMEM((remote,), jnp.int32),
            pltpu.SMEM((remote,), jnp.int32),
            pltpu.SMEM((remote,), jnp.int32),
            pltpu.VMEM(tiles.shape, BF16),
            pltpu.VMEM((remote, size, width), BF16),
            pltpu.VMEM((remote, size, width), BF16),
            pltpu.VMEM((remote, 2 * size + TAG, width // 2), BF16),
            pltpu.VMEM((2 * size + TAG, width // 2), BF16),
            pltpu.SMEM((peers,), jnp.int32),
            pltpu.SemaphoreType.DMA((2, remote)),
            pltpu.SemaphoreType.DMA((4,)),
            pltpu.SemaphoreType.DMA((peers + remote,)),
        ],
        compiler_params=params(60),
        name="pack",
    )(*in_hbm(rows, owner, cols, preact, cotangent, tiles))


def fold(x):
    half = x.shape[1] // 2
    return jnp.concatenate([x[:, :half], x[:, half:]], axis=0)


def unfold(x):
    half = x.shape[0] // 2
    return jnp.concatenate([x[:half], x[half:]], axis=1)


def two_terms(x):
    high = x.astype(BF16)
    return high, (x - high.astype(F32)).astype(BF16)


def first_kernel(group, scale, core_ref, feat, preact, cotangent, mine, other, x, pre, cot, total, came):
    width = feat.shape[1]
    span = feat.shape[0] // group

    def arrive(i):
        at = pl.ds(pl.multiple_of(i * span, span), span)
        return (
            pltpu.make_async_copy(feat.at[at], x.at[at], came.at[0, i]),
            pltpu.make_async_copy(preact.at[at], pre.at[at], came.at[1, i]),
            pltpu.make_async_copy(cotangent.at[at], cot.at[at], came.at[2, i]),
        )

    def start(i):
        for copy in arrive(i):
            copy.start()

    loop(group, start)
    total[...] = jnp.zeros_like(total)

    def step(i, _):
        at = pl.ds(pl.multiple_of(i * span, span), span)
        for copy in arrive(i):
            copy.wait()
        grad = jnp.where(pre[at] > 0, cot[at], jnp.zeros((span, width), BF16))
        total[...] += dot_tn(x[at], grad)
        return 0

    lax.fori_loop(0, group, step, 0)
    half = width // 2
    low = fold(total[:half] * scale)
    high = fold(total[half:] * scale)

    @pl.when(core_ref[0] == 0)
    def _():
        mine[...] = low
        other[...] = high

    @pl.when(core_ref[0] != 0)
    def _():
        mine[...] = high
        other[...] = low


def first_sum(scale, core, feat, preact, cotangent):
    nodes, width = feat.shape
    group = 8
    return pl.pallas_call(
        functools.partial(first_kernel, group, scale),
        out_shape=(pltpu.VMEM((width, width // 2), F32),) * 2,
        in_specs=[SMEM, HBM, HBM, HBM],
        out_specs=(VMEM, VMEM),
        scratch_shapes=[
            pltpu.VMEM((nodes, width), BF16),
            pltpu.VMEM((nodes, width), BF16),
            pltpu.VMEM((nodes, width), BF16),
            pltpu.VMEM((width, width), F32),
            pltpu.SemaphoreType.DMA((3, group)),
        ],
        compiler_params=params(60),
        cost_estimate=pl.CostEstimate(
            flops=2 * nodes * width * width,
            bytes_accessed=nodes * width * 6,
            transcendentals=0,
        ),
        name="first_sum",
    )(core, *in_hbm(feat, preact, cotangent))


def local_kernel(group, part, scale, feat, preact, cotangent, diag, weight, *refs):
    base, nodes, turned, sums, x, pre, cot, tiles, full, rounded, total, came, left = refs[3 * part :]
    width = feat.shape[1]
    size = diag.shape[1]
    span = group * size
    steps = x.shape[0] // span
    origin = part * steps

    def here(i):
        return pl.ds(pl.multiple_of(i * span, span), span)

    def there(i):
        return here(origin + i)

    def arrive(i):
        some, same = pl.ds((origin + i) * group, group), pl.ds(i * group, group)
        return (
            pltpu.make_async_copy(preact.at[there(i)], pre.at[here(i)], came.at[0, i]),
            pltpu.make_async_copy(cotangent.at[there(i)], cot.at[here(i)], came.at[1, i]),
            pltpu.make_async_copy(diag.at[some], tiles.at[same], came.at[2, i]),
            pltpu.make_async_copy(feat.at[there(i)], x.at[here(i)], came.at[3, i]),
        )

    def leave(i):
        return (
            pltpu.make_async_copy(full.at[here(i)], base.at[there(i)], left.at[0, i]),
            pltpu.make_async_copy(rounded.at[here(i)], nodes.at[there(i)], left.at[1, i]),
        )

    def start(i):
        for copy in arrive(i):
            copy.start()

    loop(steps, start)
    total[...] = refs[0][...] if part else jnp.zeros_like(total)

    def step(i):
        at = here(i)
        for copy in arrive(i):
            copy.wait()
        grad = jnp.where(pre[at] > 0, cot[at], jnp.zeros((span, width), BF16))
        parts = [
            dot_tn(tiles[i * group + b], grad[b * size : (b + 1) * size]) for b in range(group)
        ]
        high, low = two_terms(jnp.concatenate(parts, axis=0))
        w_first, w_second = weight[:width], weight[width:]
        own = dot_nt(grad, w_first) + (dot_nt(high, w_second) + dot_nt(low, w_second))
        full[at] = own
        rounded[at] = own.astype(BF16)
        columns = x[at].T
        for b in range(group):
            turned[i * group + b] = columns[:, b * size : (b + 1) * size]
        for copy in leave(i):
            copy.start()
        total[...] += jnp.dot(columns, high, preferred_element_type=F32) + jnp.dot(
            columns, low, preferred_element_type=F32
        )

    lax.fori_loop(0, steps, lambda i, _: (step(i), 0)[1], 0)
    sums[...] = total[...] * scale if part else total[...]

    def drain(i):
        for copy in leave(i):
            copy.wait()

    loop(steps, drain)


def local_work(scale, feat, preact, cotangent, diag, weight, *state):
    part = 1 if state else 0
    rows, width = feat.shape
    blocks, size, _ = diag.shape
    group = math.gcd(blocks // 2, 4)
    steps = blocks // 2 // group
    return pl.pallas_call(
        functools.partial(local_kernel, group, part, scale),
        out_shape=(
            pltpu.HBM((rows, width), F32),
            pltpu.HBM((rows, width), BF16),
            pltpu.VMEM((blocks // 2, width, size), BF16),
            pltpu.VMEM((width, width), F32),
        ),
        in_specs=[HBM, HBM, HBM, HBM, VMEM] + [VMEM, HBM, HBM][: len(state)],
        out_specs=(HBM, HBM, VMEM, VMEM),
        scratch_shapes=[
            pltpu.VMEM((rows // 2, width), BF16),
            pltpu.VMEM((rows // 2, width), BF16),
            pltpu.VMEM((rows // 2, width), BF16),
            pltpu.VMEM((blocks // 2, size, size), BF16),
            pltpu.VMEM((rows // 2, width), F32),
            pltpu.VMEM((rows // 2, width), BF16),
            pltpu.VMEM((width, width), F32),
            pltpu.SemaphoreType.DMA((4, steps)),
            pltpu.SemaphoreType.DMA((2, steps)),
        ],
        input_output_aliases={6: 0, 7: 1} if part else {},
        compiler_params=params(LOCAL_MIB),
        cost_estimate=pl.CostEstimate(
            flops=rows * width * (size + 5 * width),
            bytes_accessed=rows * width * 7 + blocks * size * size,
            transcendentals=0,
        ),
        name="local_work",
    )(*in_hbm(feat, preact, cotangent, diag), weight, *state[:1], *in_hbm(*state[1:]))


def half_sum(scale, row, ids, got, low_blocks, high_blocks, sums):
    peers = got.shape[0]
    half, width, size = low_blocks.shape
    group = math.gcd(peers, 16)
    wide = math.gcd(group, 4)
    rows = pl.ds(pl.multiple_of(row, width // 2), width // 2)

    def block(p):
        at = ids[p]
        low = low_blocks[jnp.clip(at, 0, half - 1), rows, :]
        high = high_blocks[jnp.maximum(at - half, 0), rows, :]
        return jnp.where(at < half, low, high)

    def term(step, total):
        for q in range(0, group, wide):
            pair = [step * group + q + k for k in range(wide)]
            left = jnp.concatenate([block(p) for p in pair], axis=1)
            right = jnp.concatenate([unfold(got[p, : 2 * size, :]) for p in pair], axis=0)
            total = total + jnp.dot(left, right, preferred_element_type=F32)
        return total

    total = jnp.zeros((width // 2, width), F32)
    total = lax.fori_loop(0, peers // group, term, total, unroll=peers == group)
    return fold(total * scale + sums[rows, :])


def theirs_kernel(scale, core_ref, got, low_blocks, high_blocks, sums, other, ids):
    size = low_blocks.shape[2]

    def mark(p):
        ids[p] = jnp.max(got[p, 2 * size :, :].astype(F32)).astype(jnp.int32) - 1

    loop(got.shape[0], mark)
    row = (1 - core_ref[0]) * (sums.shape[0] // 2)
    other[...] = half_sum(scale, row, ids, got, low_blocks, high_blocks, sums)


def ours_kernel(scale, core_ref, ids, got, low_blocks, high_blocks, sums, mine):
    row = core_ref[0] * (sums.shape[0] // 2)
    mine[...] = half_sum(scale, row, ids, got, low_blocks, high_blocks, sums)


def arrived(core, got, low_blocks, high_blocks, sums, scale):
    peers = got.shape[0]
    _, width, size = low_blocks.shape
    return pl.pallas_call(
        functools.partial(theirs_kernel, scale),
        out_shape=(
            pltpu.VMEM((width, width // 2), F32),
            jax.ShapeDtypeStruct((peers,), jnp.int32),
        ),
        in_specs=[SMEM, VMEM, VMEM, VMEM, VMEM],
        out_specs=(VMEM, SMEM),
        compiler_params=params(8 + peers * size * width * 5 / MIB),
        name="arrived",
    )(core, got, low_blocks, high_blocks, sums)


def own_half(core, ids, got, low_blocks, high_blocks, sums, scale):
    peers = got.shape[0]
    _, width, size = low_blocks.shape
    return pl.pallas_call(
        functools.partial(ours_kernel, scale),
        out_shape=pltpu.VMEM((width, width // 2), F32),
        in_specs=[SMEM, SMEM, VMEM, VMEM, VMEM, VMEM],
        out_specs=VMEM,
        compiler_params=params(8 + peers * size * width * 5 / MIB),
        name="own_half",
    )(core, ids, got, low_blocks, high_blocks, sums)


def finish_kernel(
    ids, got, weight, base, nodes, out, near, ready, terms, last, count, before, came, left
):
    peers, size, width = near.shape
    half = width // 2

    def block(p):
        return pl.ds(pl.multiple_of(ids[p] * size, size), size)

    def read(p):
        return pltpu.make_async_copy(base.at[block(p)], near.at[p], came.at[p])

    def write(p):
        return pltpu.make_async_copy(ready.at[p], out.at[block(p)], left.at[p])

    def writes(p):
        return (ids[p] >= 0) & (last[ids[p] + 1] == p)

    def start(p):
        @pl.when(ids[p] >= 0)
        def _():
            read(p).start()

    loop(peers, start)

    def clear(b):
        last[b] = -1
        count[b] = 0

    loop(last.shape[0], clear)

    def tally(p):
        before[p] = last[ids[p] + 1]
        last[ids[p] + 1] = p
        count[ids[p] + 1] += 1

    loop(peers, tally)

    group = math.gcd(peers, 16)

    def product(step):
        at = pl.ds(step * group, group)
        tile = jnp.concatenate([got[at, :size, :], got[at, size : 2 * size, :]], axis=2)
        tile = tile.reshape(group * size, width)
        terms[at] = dot_nt(tile, weight[...]).reshape(group, size, width)

    loop(peers // group, product)

    def one(p):
        @pl.when(ids[p] >= 0)
        def _():
            read(p).wait()

        @pl.when(writes(p))
        def _():
            def add(_, q):
                near[p] += terms[q]
                return before[q]

            lax.fori_loop(1, count[ids[p] + 1], add, before[p])
            ready[p] = (near[p] + terms[p]).astype(BF16)
            write(p).start()

    def drain(p):
        @pl.when(writes(p))
        def _():
            write(p).wait()

    loop(peers, one)
    loop(peers, drain)


def finish(ids, got, weight, base, nodes, size):
    peers = got.shape[0]
    width = base.shape[1]
    return pl.pallas_call(
        finish_kernel,
        out_shape=pltpu.HBM(nodes.shape, BF16),
        in_specs=[SMEM, VMEM, VMEM, HBM, HBM],
        out_specs=HBM,
        scratch_shapes=[
            pltpu.VMEM((peers, size, width), F32),
            pltpu.VMEM((peers, size, width), BF16),
            pltpu.VMEM((peers, size, width), F32),
            pltpu.SMEM((nodes.shape[0] // size + 1,), jnp.int32),
            pltpu.SMEM((nodes.shape[0] // size + 1,), jnp.int32),
            pltpu.SMEM((peers,), jnp.int32),
            pltpu.SemaphoreType.DMA((peers,)),
            pltpu.SemaphoreType.DMA((peers,)),
        ],
        input_output_aliases={4: 0},
        compiler_params=params(6 + peers * size * width * 12 / MIB),
        cost_estimate=pl.CostEstimate(
            flops=2 * peers * size * width * width,
            bytes_accessed=peers * size * width * 8,
            transcendentals=0,
        ),
        name="finish",
    )(ids, got, weight[width:], *in_hbm(base, nodes))


def swap(x, bit, peers):
    return lax.ppermute(x, "rows", [(i, i ^ bit) for i in range(peers)])


def widen(total, core, peers):
    there = swap(total, 1, peers)
    low, high = jnp.where(core == 0, total, there), jnp.where(core == 0, there, total)
    half = total.shape[0] // 2
    return [jnp.concatenate([x[:half], x[half:]], axis=1) for x in (low, high)]


def exchange(total, bit, peers):
    return total + swap(total.astype(BF16), bit, peers).astype(F32)


def local(
    node_features,
    preact,
    cotangent,
    weight,
    diag_tiles,
    edge_tiles,
    entry_rows,
    entry_owner,
    entry_cols,
):
    blocks, size, _ = diag_tiles.shape
    peers = lax.axis_size("rows")
    if peers & (peers - 1):
        raise ValueError("rows")
    core = lax.axis_index("rows") & 1
    which = core.reshape(1).astype(jnp.int32)
    scale = 1.0 / math.sqrt(peers * blocks * size)
    bits = [1 << i for i in range(1, peers.bit_length() - 1)]
    packed = pack(
        preact, cotangent, edge_tiles, entry_rows, entry_owner.reshape(-1), entry_cols, peers
    )
    got = lax.all_to_all(packed, "rows", split_axis=0, concat_axis=0, tiled=True)

    mine, other = first_sum(scale, which, node_features, preact, cotangent)
    first = mine + swap(other, 1, peers)
    arrays = (node_features, preact, cotangent, diag_tiles, weight)
    base, nodes, low_blocks, sums = local_work(scale, *arrays)
    for bit in bits[:-1]:
        first = exchange(first, bit, peers)
        if bit == 2:
            first, sums = lax.optimization_barrier((first, sums))
    base, nodes, high_blocks, sums = local_work(scale, *arrays, sums, base, nodes)
    sent = first.astype(BF16)
    sent, sums = lax.optimization_barrier((sent, sums))

    sent, got = lax.optimization_barrier((sent, got))
    other, ids = arrived(which, got, low_blocks, high_blocks, sums, scale)
    mine = own_half(which, ids, got, low_blocks, high_blocks, sums, scale)
    second = mine + swap(other, 1, peers)
    first = sent.astype(F32) + swap(sent, bits[-1], peers).astype(F32)
    for bit in bits[:-1]:
        second = exchange(second, bit, peers)
    tied, second = lax.optimization_barrier((ids, second))
    nodes = finish(tied, got, weight, base, nodes, size)
    for bit in bits[-1:]:
        second = exchange(second, bit, peers)
    second, nodes = lax.optimization_barrier((second, nodes))
    rows = widen(first, core, peers) + widen(second, core, peers)
    return nodes, jnp.concatenate(rows, axis=0)


def solution(mesh):
    in_specs = (
        P(("parts", "rows"), None),
        P(("parts", "rows"), None),
        P(("parts", "rows"), None),
        P(),
        P(("parts", "rows"), None, None),
        P(("parts", "rows"), None, None),
        P(("parts", "rows")),
        P(("parts", "rows"), None),
        P(("parts", "rows")),
    )
    out_specs = (P(("parts", "rows"), None), P("parts", None))
    return jax.shard_map(local, mesh=mesh, in_specs=in_specs, out_specs=out_specs, check_vma=False)
```

```python
import functools
import math

import jax
import jax.numpy as jnp
from jax import lax
from jax.experimental import pallas as pl
from jax.experimental.pallas import tpu as pltpu
from jax.sharding import PartitionSpec as P

F32 = jnp.float32
BF16 = jnp.bfloat16
MIB = 1024 * 1024
TAG = 16
PACK_GROUP = 4
LOCAL_MIB = 58

VMEM = pl.BlockSpec(memory_space=pltpu.VMEM)
SMEM = pl.BlockSpec(memory_space=pltpu.SMEM)
HBM = pl.BlockSpec(memory_space=pltpu.HBM)


def in_hbm(*arrays):
    return [pltpu.with_memory_space_constraint(x, pltpu.HBM) for x in arrays]


def params(mib):
    return pltpu.CompilerParams(vmem_limit_bytes=int(mib * MIB))


def loop(count, body):
    lax.fori_loop(0, count, lambda i, _: (body(i), 0)[1], 0, unroll=count <= 16)


def dot_tn(a, b):
    return lax.dot_general(a, b, (((0,), (0,)), ((), ())), preferred_element_type=F32)


def dot_nt(a, b):
    return lax.dot_general(a, b, (((1,), (1,)), ((), ())), preferred_element_type=F32)


def pack_kernel(
    rows, owner, cols, preact, cotangent, tiles, out,
    rows_ref, owner_ref, cols_ref, held, pre, cot, ready, blank, used, sems, late, left,
):
    remote, size, width = pre.shape
    peers = out.shape[0]
    half = width // 2
    lists = [
        pltpu.make_async_copy(source, target, late.at[i])
        for i, (source, target) in enumerate(
            ((rows, rows_ref), (owner, owner_ref), (cols, cols_ref), (tiles, held))
        )
    ]
    for copy in lists:
        copy.start()
    blank[...] = jnp.zeros_like(blank)

    def unused(p):
        used[p] = 0

    loop(peers, unused)
    lists[0].wait()

    def fetch(k):
        block = pl.ds(pl.multiple_of(rows_ref[k] * size, size), size)
        return (
            pltpu.make_async_copy(preact.at[block], pre.at[k], sems.at[0, k]),
            pltpu.make_async_copy(cotangent.at[block], cot.at[k], sems.at[1, k]),
        )

    def start(k):
        for copy in fetch(k):
            copy.start()

    loop(remote, start)
    for copy in lists[1:]:
        copy.wait()

    def turn(k):
        held[k] = held[k].T

    loop(remote, turn)

    def mark(k):
        used[owner_ref[k]] = 1

    loop(remote, mark)

    def clear(p):
        return pltpu.make_async_copy(blank, out.at[p], left.at[p])

    def send(k):
        return pltpu.make_async_copy(ready.at[k], out.at[owner_ref[k]], left.at[peers + k])

    def start_clear(p):
        @pl.when(used[p] == 0)
        def _():
            clear(p).start()

    loop(peers, start_clear)

    def product(k):
        grad = jnp.where(pre[k] > 0, cot[k], jnp.zeros_like(cot[k]))
        term = jnp.dot(held[k], grad, preferred_element_type=F32).astype(BF16)
        ready[k, 0:size, :] = term[:, :half]
        ready[k, size : 2 * size, :] = term[:, half:]
        tag = (cols_ref[k] + 1).astype(F32)
        ready[k, 2 * size :, :] = jnp.full((TAG, half), tag, F32).astype(BF16)

    group = math.gcd(remote, PACK_GROUP)

    def batch(step):
        for k in range(group):
            for copy in fetch(step * group + k):
                copy.wait()
        for k in range(group):
            product(step * group + k)
        for k in range(group):
            send(step * group + k).start()

    loop(remote // group, batch)

    def end_clear(p):
        @pl.when(used[p] == 0)
        def _():
            clear(p).wait()

    loop(peers, end_clear)
    loop(remote, lambda k: send(k).wait())


def pack(preact, cotangent, tiles, rows, owner, cols, peers):
    remote, size, _ = tiles.shape
    width = preact.shape[1]
    return pl.pallas_call(
        pack_kernel,
        out_shape=jax.ShapeDtypeStruct((peers, 2 * size + TAG, width // 2), BF16),
        in_specs=[HBM] * 6,
        out_specs=HBM,
        scratch_shapes=[
            pltpu.SMEM((remote,), jnp.int32),
            pltpu.SMEM((remote,), jnp.int32),
            pltpu.SMEM((remote,), jnp.int32),
            pltpu.VMEM(tiles.shape, BF16),
            pltpu.VMEM((remote, size, width), BF16),
            pltpu.VMEM((remote, size, width), BF16),
            pltpu.VMEM((remote, 2 * size + TAG, width // 2), BF16),
            pltpu.VMEM((2 * size + TAG, width // 2), BF16),
            pltpu.SMEM((peers,), jnp.int32),
            pltpu.SemaphoreType.DMA((2, remote)),
            pltpu.SemaphoreType.DMA((4,)),
            pltpu.SemaphoreType.DMA((peers + remote,)),
        ],
        compiler_params=params(60),
        name="pack",
    )(*in_hbm(rows, owner, cols, preact, cotangent, tiles))


def fold(x):
    half = x.shape[1] // 2
    return jnp.concatenate([x[:, :half], x[:, half:]], axis=0)


def unfold(x):
    half = x.shape[0] // 2
    return jnp.concatenate([x[:half], x[half:]], axis=1)


def two_terms(x):
    high = x.astype(BF16)
    return high, (x - high.astype(F32)).astype(BF16)


def first_kernel(group, scale, core_ref, feat, preact, cotangent, mine, other, x, pre, cot, total, came):
    width = feat.shape[1]
    span = feat.shape[0] // group

    def arrive(i):
        at = pl.ds(pl.multiple_of(i * span, span), span)
        return (
            pltpu.make_async_copy(feat.at[at], x.at[at], came.at[0, i]),
            pltpu.make_async_copy(preact.at[at], pre.at[at], came.at[1, i]),
            pltpu.make_async_copy(cotangent.at[at], cot.at[at], came.at[2, i]),
        )

    def start(i):
        for copy in arrive(i):
            copy.start()

    loop(group, start)
    total[...] = jnp.zeros_like(total)

    def step(i, _):
        at = pl.ds(pl.multiple_of(i * span, span), span)
        for copy in arrive(i):
            copy.wait()
        grad = jnp.where(pre[at] > 0, cot[at], jnp.zeros((span, width), BF16))
        total[...] += dot_tn(x[at], grad)
        return 0

    lax.fori_loop(0, group, step, 0)
    half = width // 2
    low = fold(total[:half] * scale)
    high = fold(total[half:] * scale)

    @pl.when(core_ref[0] == 0)
    def _():
        mine[...] = low
        other[...] = high

    @pl.when(core_ref[0] != 0)
    def _():
        mine[...] = high
        other[...] = low


def first_sum(scale, core, feat, preact, cotangent):
    nodes, width = feat.shape
    group = 8
    return pl.pallas_call(
        functools.partial(first_kernel, group, scale),
        out_shape=(pltpu.VMEM((width, width // 2), F32),) * 2,
        in_specs=[SMEM, HBM, HBM, HBM],
        out_specs=(VMEM, VMEM),
        scratch_shapes=[
            pltpu.VMEM((nodes, width), BF16),
            pltpu.VMEM((nodes, width), BF16),
            pltpu.VMEM((nodes, width), BF16),
            pltpu.VMEM((width, width), F32),
            pltpu.SemaphoreType.DMA((3, group)),
        ],
        compiler_params=params(60),
        cost_estimate=pl.CostEstimate(
            flops=2 * nodes * width * width,
            bytes_accessed=nodes * width * 6,
            transcendentals=0,
        ),
        name="first_sum",
    )(core, *in_hbm(feat, preact, cotangent))


def local_kernel(group, part, scale, feat, preact, cotangent, diag, weight, *refs):
    base, nodes, turned, sums, x, pre, cot, tiles, full, rounded, total, came, left = refs[3 * part :]
    width = feat.shape[1]
    size = diag.shape[1]
    span = group * size
    steps = x.shape[0] // span
    origin = part * steps

    def here(i):
        return pl.ds(pl.multiple_of(i * span, span), span)

    def there(i):
        return here(origin + i)

    def arrive(i):
        some, same = pl.ds((origin + i) * group, group), pl.ds(i * group, group)
        return (
            pltpu.make_async_copy(preact.at[there(i)], pre.at[here(i)], came.at[0, i]),
            pltpu.make_async_copy(cotangent.at[there(i)], cot.at[here(i)], came.at[1, i]),
            pltpu.make_async_copy(diag.at[some], tiles.at[same], came.at[2, i]),
            pltpu.make_async_copy(feat.at[there(i)], x.at[here(i)], came.at[3, i]),
        )

    def leave(i):
        return (
            pltpu.make_async_copy(full.at[here(i)], base.at[there(i)], left.at[0, i]),
            pltpu.make_async_copy(rounded.at[here(i)], nodes.at[there(i)], left.at[1, i]),
        )

    def start(i):
        for copy in arrive(i):
            copy.start()

    loop(steps, start)
    total[...] = refs[0][...] if part else jnp.zeros_like(total)

    def step(i):
        at = here(i)
        for copy in arrive(i):
            copy.wait()
        grad = jnp.where(pre[at] > 0, cot[at], jnp.zeros((span, width), BF16))
        parts = [
            dot_tn(tiles[i * group + b], grad[b * size : (b + 1) * size]) for b in range(group)
        ]
        high, low = two_terms(jnp.concatenate(parts, axis=0))
        w_first, w_second = weight[:width], weight[width:]
        own = dot_nt(grad, w_first) + (dot_nt(high, w_second) + dot_nt(low, w_second))
        full[at] = own
        rounded[at] = own.astype(BF16)
        columns = x[at].T
        for b in range(group):
            turned[i * group + b] = columns[:, b * size : (b + 1) * size]
        for copy in leave(i):
            copy.start()
        total[...] += jnp.dot(columns, high, preferred_element_type=F32) + jnp.dot(
            columns, low, preferred_element_type=F32
        )

    lax.fori_loop(0, steps, lambda i, _: (step(i), 0)[1], 0)
    sums[...] = total[...] * scale if part else total[...]

    def drain(i):
        for copy in leave(i):
            copy.wait()

    loop(steps, drain)


def local_work(scale, feat, preact, cotangent, diag, weight, *state):
    part = 1 if state else 0
    rows, width = feat.shape
    blocks, size, _ = diag.shape
    group = math.gcd(blocks // 2, 4)
    steps = blocks // 2 // group
    return pl.pallas_call(
        functools.partial(local_kernel, group, part, scale),
        out_shape=(
            pltpu.HBM((rows, width), F32),
            pltpu.HBM((rows, width), BF16),
            pltpu.VMEM((blocks // 2, width, size), BF16),
            pltpu.VMEM((width, width), F32),
        ),
        in_specs=[HBM, HBM, HBM, HBM, VMEM] + [VMEM, HBM, HBM][: len(state)],
        out_specs=(HBM, HBM, VMEM, VMEM),
        scratch_shapes=[
            pltpu.VMEM((rows // 2, width), BF16),
            pltpu.VMEM((rows // 2, width), BF16),
            pltpu.VMEM((rows // 2, width), BF16),
            pltpu.VMEM((blocks // 2, size, size), BF16),
            pltpu.VMEM((rows // 2, width), F32),
            pltpu.VMEM((rows // 2, width), BF16),
            pltpu.VMEM((width, width), F32),
            pltpu.SemaphoreType.DMA((4, steps)),
            pltpu.SemaphoreType.DMA((2, steps)),
        ],
        input_output_aliases={6: 0, 7: 1} if part else {},
        compiler_params=params(LOCAL_MIB),
        cost_estimate=pl.CostEstimate(
            flops=rows * width * (size + 5 * width),
            bytes_accessed=rows * width * 7 + blocks * size * size,
            transcendentals=0,
        ),
        name="local_work",
    )(*in_hbm(feat, preact, cotangent, diag), weight, *state[:1], *in_hbm(*state[1:]))


def half_sum(scale, row, ids, got, low_blocks, high_blocks, sums):
    peers = got.shape[0]
    half, width, size = low_blocks.shape
    group = math.gcd(peers, 16)
    wide = math.gcd(group, 4)
    rows = pl.ds(pl.multiple_of(row, width // 2), width // 2)

    def block(p):
        at = ids[p]
        low = low_blocks[jnp.clip(at, 0, half - 1), rows, :]
        high = high_blocks[jnp.maximum(at - half, 0), rows, :]
        return jnp.where(at < half, low, high)

    def term(step, total):
        for q in range(0, group, wide):
            pair = [step * group + q + k for k in range(wide)]
            left = jnp.concatenate([block(p) for p in pair], axis=1)
            right = jnp.concatenate([unfold(got[p, : 2 * size, :]) for p in pair], axis=0)
            total = total + jnp.dot(left, right, preferred_element_type=F32)
        return total

    total = jnp.zeros((width // 2, width), F32)
    if peers == group:
        total = term(0, total)
    else:
        total = lax.fori_loop(0, peers // group, term, total)
    return fold(total * scale + sums[rows, :])


def theirs_kernel(scale, core_ref, got, low_blocks, high_blocks, sums, other, ids):
    size = low_blocks.shape[2]

    def mark(p):
        at = jnp.max(got[p, 2 * size :, :].astype(F32)).astype(jnp.int32) - 1
        ids[p] = at
        return at

    peers = got.shape[0]
    if peers <= 16:
        known = [mark(p) for p in range(peers)]
    else:
        loop(peers, mark)
        known = ids
    row = (1 - core_ref[0]) * (sums.shape[0] // 2)
    other[...] = half_sum(scale, row, known, got, low_blocks, high_blocks, sums)


def ours_kernel(scale, core_ref, ids, got, low_blocks, high_blocks, sums, mine):
    row = core_ref[0] * (sums.shape[0] // 2)
    mine[...] = half_sum(scale, row, ids, got, low_blocks, high_blocks, sums)


def arrived(core, got, low_blocks, high_blocks, sums, scale):
    peers = got.shape[0]
    _, width, size = low_blocks.shape
    return pl.pallas_call(
        functools.partial(theirs_kernel, scale),
        out_shape=(
            pltpu.VMEM((width, width // 2), F32),
            jax.ShapeDtypeStruct((peers,), jnp.int32),
        ),
        in_specs=[SMEM, VMEM, VMEM, VMEM, VMEM],
        out_specs=(VMEM, SMEM),
        compiler_params=params(8 + peers * size * width * 5 / MIB),
        name="arrived",
    )(core, got, low_blocks, high_blocks, sums)


def own_half(core, ids, got, low_blocks, high_blocks, sums, scale):
    peers = got.shape[0]
    _, width, size = low_blocks.shape
    return pl.pallas_call(
        functools.partial(ours_kernel, scale),
        out_shape=pltpu.VMEM((width, width // 2), F32),
        in_specs=[SMEM, SMEM, VMEM, VMEM, VMEM, VMEM],
        out_specs=VMEM,
        compiler_params=params(8 + peers * size * width * 5 / MIB),
        name="own_half",
    )(core, ids, got, low_blocks, high_blocks, sums)


def finish_kernel(
    ids, got, weight, base, nodes, out, near, ready, terms, last, count, before, came, left
):
    peers, size, width = near.shape
    half = width // 2

    def block(p):
        return pl.ds(pl.multiple_of(ids[p] * size, size), size)

    def read(p):
        return pltpu.make_async_copy(base.at[block(p)], near.at[p], came.at[p])

    def write(p):
        return pltpu.make_async_copy(ready.at[p], out.at[block(p)], left.at[p])

    def writes(p):
        return (ids[p] >= 0) & (last[ids[p] + 1] == p)

    def start(p):
        @pl.when(ids[p] >= 0)
        def _():
            read(p).start()

    loop(peers, start)

    def clear(b):
        last[b] = -1
        count[b] = 0

    loop(last.shape[0], clear)

    def tally(p):
        before[p] = last[ids[p] + 1]
        last[ids[p] + 1] = p
        count[ids[p] + 1] += 1

    loop(peers, tally)

    group = math.gcd(peers, 16)

    def product(step):
        at = pl.ds(step * group, group)
        tile = jnp.concatenate([got[at, :size, :], got[at, size : 2 * size, :]], axis=2)
        tile = tile.reshape(group * size, width)
        terms[at] = dot_nt(tile, weight[...]).reshape(group, size, width)

    loop(peers // group, product)

    def one(p):
        @pl.when(ids[p] >= 0)
        def _():
            read(p).wait()

        @pl.when(writes(p))
        def _():
            def add(_, q):
                near[p] += terms[q]
                return before[q]

            lax.fori_loop(1, count[ids[p] + 1], add, before[p])
            ready[p] = (near[p] + terms[p]).astype(BF16)
            write(p).start()

    def drain(p):
        @pl.when(writes(p))
        def _():
            write(p).wait()

    loop(peers, one)
    loop(peers, drain)


def finish(ids, got, weight, base, nodes, size):
    peers = got.shape[0]
    width = base.shape[1]
    return pl.pallas_call(
        finish_kernel,
        out_shape=pltpu.HBM(nodes.shape, BF16),
        in_specs=[SMEM, VMEM, VMEM, HBM, HBM],
        out_specs=HBM,
        scratch_shapes=[
            pltpu.VMEM((peers, size, width), F32),
            pltpu.VMEM((peers, size, width), BF16),
            pltpu.VMEM((peers, size, width), F32),
            pltpu.SMEM((nodes.shape[0] // size + 1,), jnp.int32),
            pltpu.SMEM((nodes.shape[0] // size + 1,), jnp.int32),
            pltpu.SMEM((peers,), jnp.int32),
            pltpu.SemaphoreType.DMA((peers,)),
            pltpu.SemaphoreType.DMA((peers,)),
        ],
        input_output_aliases={4: 0},
        compiler_params=params(6 + peers * size * width * 12 / MIB),
        cost_estimate=pl.CostEstimate(
            flops=2 * peers * size * width * width,
            bytes_accessed=peers * size * width * 8,
            transcendentals=0,
        ),
        name="finish",
    )(ids, got, weight[width:], *in_hbm(base, nodes))


def swap(x, bit, peers):
    return lax.ppermute(x, "rows", [(i, i ^ bit) for i in range(peers)])


def widen(total, core, peers):
    there = swap(total, 1, peers)
    low, high = jnp.where(core == 0, total, there), jnp.where(core == 0, there, total)
    half = total.shape[0] // 2
    return [jnp.concatenate([x[:half], x[half:]], axis=1) for x in (low, high)]


def exchange(total, bit, peers):
    return total + swap(total.astype(BF16), bit, peers).astype(F32)


def local(
    node_features,
    preact,
    cotangent,
    weight,
    diag_tiles,
    edge_tiles,
    entry_rows,
    entry_owner,
    entry_cols,
):
    blocks, size, _ = diag_tiles.shape
    peers = lax.axis_size("rows")
    if peers & (peers - 1):
        raise ValueError("rows")
    core = lax.axis_index("rows") & 1
    which = core.reshape(1).astype(jnp.int32)
    scale = 1.0 / math.sqrt(peers * blocks * size)
    bits = [1 << i for i in range(1, peers.bit_length() - 1)]
    packed = pack(
        preact, cotangent, edge_tiles, entry_rows, entry_owner.reshape(-1), entry_cols, peers
    )
    got = lax.all_to_all(packed, "rows", split_axis=0, concat_axis=0, tiled=True)

    mine, other = first_sum(scale, which, node_features, preact, cotangent)
    first = mine + swap(other, 1, peers)
    arrays = (node_features, preact, cotangent, diag_tiles, weight)
    base, nodes, low_blocks, sums = local_work(scale, *arrays)
    for bit in bits[:-1]:
        first = exchange(first, bit, peers)
        if bit == 2:
            first, sums = lax.optimization_barrier((first, sums))
    base, nodes, high_blocks, sums = local_work(scale, *arrays, sums, base, nodes)
    sent = first.astype(BF16)
    sent, sums = lax.optimization_barrier((sent, sums))

    sent, got = lax.optimization_barrier((sent, got))
    other, ids = arrived(which, got, low_blocks, high_blocks, sums, scale)
    mine = own_half(which, ids, got, low_blocks, high_blocks, sums, scale)
    second = mine + swap(other, 1, peers)
    first = sent.astype(F32) + swap(sent, bits[-1], peers).astype(F32)
    for bit in bits[:-1]:
        second = exchange(second, bit, peers)
    tied, second = lax.optimization_barrier((ids, second))
    nodes = finish(tied, got, weight, base, nodes, size)
    for bit in bits[-1:]:
        second = exchange(second, bit, peers)
    second, nodes = lax.optimization_barrier((second, nodes))
    rows = widen(first, core, peers) + widen(second, core, peers)
    return nodes, jnp.concatenate(rows, axis=0)


def solution(mesh):
    in_specs = (
        P(("parts", "rows"), None),
        P(("parts", "rows"), None),
        P(("parts", "rows"), None),
        P(),
        P(("parts", "rows"), None, None),
        P(("parts", "rows"), None, None),
        P(("parts", "rows")),
        P(("parts", "rows"), None),
        P(("parts", "rows")),
    )
    out_specs = (P(("parts", "rows"), None), P("parts", None))
    return jax.shard_map(local, mesh=mesh, in_specs=in_specs, out_specs=out_specs, check_vma=False)
```
